256 devices in a mesh: member: 8 (over x, y_hi), fsdp: 32 (over z, y_lo, core).
Axes of the slice: x: 4, y: 4 (y_hi: 2, y_lo: 2; y = y_hi * 2 + y_lo), z: 8, core: 2. Of those that a mesh axis runs over, the one named last changes fastest.
Arguments:
- tokens: bfloat16 [8, 4096, 1792], P('member', 'fsdp'), may hold values from -6 to 6
- cotangent: bfloat16 [8, 4096, 7168], P('member', 'fsdp'), may hold values from -8 to 8
- gate_weight: bfloat16 [8, 7168, 1792], P('member', 'fsdp'), may hold values from -5 to 5
- up_weight: bfloat16 [8, 7168, 1792], P('member', 'fsdp'), may hold values from -5 to 5
- gate_first: bfloat16 [8, 7168, 1792], P('member', 'fsdp'), may hold values from -4 to 4
- up_first: bfloat16 [8, 7168, 1792], P('member', 'fsdp'), may hold values from -4 to 4
- gate_second: bfloat16 [8, 7168, 1792], P('member', 'fsdp'), may hold values from 0.19921875 to 4
- up_second: bfloat16 [8, 7168, 1792], P('member', 'fsdp'), may hold values from 0.19921875 to 4
- winner: int32 [8], replicated, may hold values from 0 to 7, as said below
- rate_index: int32 [8], replicated, may hold values from 0 to 4
Outputs:
- new_gate: bfloat16 [8, 7168, 1792], P('member', 'fsdp')
- new_up: bfloat16 [8, 7168, 1792], P('member', 'fsdp')
- new_gate_first: bfloat16 [8, 7168, 1792], P('member', 'fsdp')
- new_up_first: bfloat16 [8, 7168, 1792], P('member', 'fsdp')
- new_gate_second: bfloat16 [8, 7168, 1792], P('member', 'fsdp')
- new_up_second: bfloat16 [8, 7168, 1792], P('member', 'fsdp')
The draws below stay inside these ranges and needn't reach their ends.
Inputs may be any that keep to these rules, and one draw needn't show every extreme that they name: Exactly 2 members m have winner[m] != m; for those, winner[m] is a member whose own winner is itself. One winner may serve several of them.
All inputs are finite; a program needn't handle non-finite values.
Results may differ from the reference program's by a relative error of at most 0.003.
Values may be sent and summed in bfloat16 or wider, within the bound.
No kernel may reach another device: no remote copies, remote signals or barrier semaphores. Data moves between devices by JAX's collectives and lax.ppermute only.
A program may use at most 128 MiB of HBM per device.

```python
import math
import jax
import jax.numpy as jnp
from jax import lax

D = 1792
FF = 7168
TOKENS = 4096
MEMBERS = 8
LOSERS = 2


def draw_winner(key, part):
    key = jax.random.fold_in(key, 11)
    key_rank, key_pick = jax.random.split(key)
    ranking = jax.random.permutation(key_rank, MEMBERS).astype(jnp.int32)
    picks = jax.random.randint(key_pick, (LOSERS,), 0, LOSERS).astype(jnp.int32)
    leaders = ranking[:LOSERS]
    trailing = ranking[MEMBERS - LOSERS:]
    base = jnp.arange(MEMBERS, dtype=jnp.int32)
    return base.at[trailing].set(leaders[picks]).astype(jnp.int32)


def set_ends(result, rng, low, largest):
    shape = result.shape
    place = [jax.random.randint(jax.random.fold_in(rng, axis), (), 0, shape[axis]) for axis in range(len(shape))]
    result = result.at[tuple(place)].set(low)
    longest = shape.index(max(shape))
    place[longest] = (place[longest] + 1) % shape[longest]
    return result.at[tuple(place)].set(largest)


def spiked(array, own_key, source, target, parts, factor):
    owner, partner = [(jnp.arange(array.shape[position]) // (array.shape[position] // parts)).reshape([-1 if axis == position else 1 for axis in range(array.ndim)]) for position in (source, target)]
    chosen = jax.random.permutation(own_key, parts)[partner]
    strong = (owner == chosen) | (owner == (partner + parts // 2) % parts)
    return jnp.where(strong, factor * array, array)


def block_scale(stream_key, dims, cuts, low, largest):
    factor_of, own = 1.0, jax.random.fold_in(stream_key, 6)
    for dim, blocks in cuts:
        draws = jnp.exp(jax.random.uniform(jax.random.fold_in(own, dim), (blocks,), jnp.float32, low / len(cuts), largest / len(cuts)))
        factor_of = factor_of * jnp.repeat(draws, dims[dim] // blocks).reshape([-1 if axis == dim else 1 for axis in range(len(dims))])
    return factor_of


def scatter_about(rng, shape, width, reach, cuts=(), held_as=jnp.bfloat16):
    drawn = width * jax.random.normal(rng, shape, jnp.float32)
    if cuts:
        drawn = drawn * block_scale(rng, shape, cuts, -0.22, 0.18)
    return jnp.clip(drawn, -reach, reach).astype(held_as)


def bell_draw_with(stream_key, shape, scale, most, pieces, heavy, kind=jnp.bfloat16):
    result = scale * jax.random.normal(stream_key, shape, jnp.float32)
    if pieces:
        result = result * block_scale(stream_key, shape, pieces, -0.22, 0.18)
    return jnp.clip(spiked(result, jax.random.fold_in(stream_key, 3), *heavy), -most, most).astype(kind)


def setup_inputs(seed: int = 0) -> dict:
    keys = jax.random.split(jax.random.key(seed), 11)
    return {
        "tokens": scatter_about(keys[0], (MEMBERS, TOKENS, D), 1.0, 6.0, ((0, 8), (1, 32))),
        "cotangent": bell_draw_with(keys[1], (MEMBERS, TOKENS, FF), 1.0, 8.0, ((0, 8), (1, 32)), (1, 2, 32, 2.75)),
        "gate_weight": scatter_about(keys[2], (MEMBERS, FF, D), 1.0, 5.0, ((0, 8), (1, 32))),
        "up_weight": scatter_about(keys[3], (MEMBERS, FF, D), 1.0, 5.0, ((0, 8), (1, 32))),
        "gate_first": scatter_about(keys[4], (MEMBERS, FF, D), 0.5, 4.0, ((0, 8), (1, 32))),
        "up_first": scatter_about(keys[5], (MEMBERS, FF, D), 0.5, 4.0, ((0, 8), (1, 32))),
        "gate_second": jnp.clip(jnp.exp(math.log(4.0) - 2.9996462 * jax.random.uniform(keys[6], (MEMBERS, FF, D), jnp.float32) ** block_scale(keys[6], (MEMBERS, FF, D), ((0, 8), (1, 32)), -0.2, 0.2)), 0.19921875, 4.0).astype(jnp.bfloat16),
        "up_second": jnp.clip(jnp.exp(math.log(4.0) - 2.9996462 * jax.random.uniform(keys[7], (MEMBERS, FF, D), jnp.float32) ** block_scale(keys[7], (MEMBERS, FF, D), ((0, 8), (1, 32)), -0.2, 0.2)), 0.19921875, 4.0).astype(jnp.bfloat16),
        "winner": draw_winner(jax.random.fold_in(keys[10], 71), 0),
        "rate_index": set_ends(jax.random.randint(keys[9], (MEMBERS,), 0, 5), jax.random.fold_in(keys[9], 1), 0, 4).astype(jnp.int32),
    }


gelu_c = 0.7978845608028654
bias_first = 1.0 - 0.9 ** 10
bias_second = 1.0 - 0.95 ** 10

def gelu_parts(gate_pre):
    tangent = jnp.tanh(gelu_c * (gate_pre + 0.044715 * gate_pre * gate_pre * gate_pre))
    activated = 0.5 * gate_pre * (1.0 + tangent)
    slope = 0.5 * (1.0 + tangent) + 0.5 * gate_pre * (1.0 - tangent * tangent) * gelu_c * (1.0 + 3.0 * 0.044715 * gate_pre * gate_pre)
    return (activated, slope)

def adam_update(weight, moment_one, moment_two, grad, learning):
    first_new = 0.9 * moment_one.astype(jnp.float32) + 0.1 * grad
    second_new = 0.95 * moment_two.astype(jnp.float32) + 0.05 * grad * grad
    update = learning * (first_new / bias_first) / (jnp.sqrt(second_new / bias_second) + 1e-08)
    new_weight = weight.astype(jnp.float32) - update
    return (new_weight.astype(jnp.bfloat16), first_new.astype(jnp.bfloat16), second_new.astype(jnp.bfloat16))

def reference(tokens, cotangent, gate_weight, up_weight, gate_first, up_first, gate_second, up_second, winner, rate_index):
    scale = D ** (-0.5)

    def member_step(member):
        source = winner[member]
        gate_w = gate_weight[source]
        up_w = up_weight[source]
        own_rows = tokens[member]
        cot_f32 = cotangent[member].astype(jnp.float32)
        gate_pre = jnp.dot(own_rows, gate_w.T, preferred_element_type=jnp.float32) * scale
        up_pre = jnp.dot(own_rows, up_w.T, preferred_element_type=jnp.float32) * scale
        activated, slope = gelu_parts(gate_pre)
        gate_cot = (cot_f32 * up_pre * slope).astype(jnp.bfloat16)
        up_cot = (cot_f32 * activated).astype(jnp.bfloat16)
        gate_grad = jnp.dot(gate_cot.T, own_rows, preferred_element_type=jnp.float32) * scale
        up_grad = jnp.dot(up_cot.T, own_rows, preferred_element_type=jnp.float32) * scale
        learning = 0.2 * jnp.exp2((rate_index[member].astype(jnp.float32) - 2.0) * 0.5)
        new_gate, gate_one, gate_two = adam_update(gate_w, gate_first[source], gate_second[source], gate_grad, learning)
        new_up, up_one, up_two = adam_update(up_w, up_first[source], up_second[source], up_grad, learning)
        return (new_gate, new_up, gate_one, up_one, gate_two, up_two)
    results = lax.map(member_step, jnp.arange(MEMBERS, dtype=jnp.int32))
    return (results[0], results[1], results[2], results[3], results[4], results[5])
```

```python
import functools

import jax
import jax.numpy as jnp
from jax import lax
from jax.experimental import pallas as pl
from jax.experimental.pallas import tpu as pltpu
from jax.sharding import PartitionSpec as P

gelu_c = 0.7978845608028654
bias_first = 1.0 - 0.9**10
bias_second = 1.0 - 0.95**10
nz = 8
halves = 2


def device(z, low, core):
    return (z * 2 + low) * 2 + core


everyone = [(z, low, core) for z in range(nz) for low in range(2) for core in range(2)]
z_up = [(device(z, a, c), device((z + 1) % nz, a, c)) for z, a, c in everyone]
z_down = [(b, a) for a, b in z_up]
core_swap = [(i, i ^ 1) for i in range(32)]
low_swap = [(i, i ^ 2) for i in range(32)]


def gelu_parts(gate_pre):
    tangent = jnp.tanh(gelu_c * (gate_pre + 0.044715 * gate_pre * gate_pre * gate_pre))
    activated = 0.5 * gate_pre * (1.0 + tangent)
    slope = 0.5 * (1.0 + tangent) + 0.5 * gate_pre * (1.0 - tangent * tangent) * gelu_c * (
        1.0 + 3.0 * 0.044715 * gate_pre * gate_pre
    )
    return (activated, slope)


def block_terms(weights, token_block, cot, scale):
    half = cot.shape[0]
    pre = (
        lax.dot_general(
            weights, token_block, (((1,), (1,)), ((), ())), preferred_element_type=jnp.float32
        )
        * scale
    )
    activated, slope = gelu_parts(pre[:half])
    gate_cot = (cot * pre[half:] * slope).astype(jnp.bfloat16)
    up_cot = (cot * activated).astype(jnp.bfloat16)
    return jnp.dot(
        jnp.concatenate([gate_cot, up_cot], axis=0),
        token_block,
        preferred_element_type=jnp.float32,
    )


def step_kernel(count, first, last, scale, ids, rate, w_ref, *refs):
    tokens = refs[: 2 * count]
    cots = refs[2 * count : 6 * count]
    refs = refs[6 * count :]
    rows, width = w_ref.shape[1], w_ref.shape[2]
    weights = w_ref[...].reshape(2 * rows, width)
    total = None
    if not first:
        total = refs[0][...].reshape(2 * rows, width)
        refs = refs[1:]
    for j in range(2 * count):
        cot = jnp.concatenate([cots[2 * j][0], cots[2 * j + 1][0]], axis=1).astype(jnp.float32)
        part = block_terms(weights, tokens[j][...], cot, scale)
        total = part if total is None else total + part
    if not last:
        refs[0][...] = total.reshape(2, rows, width)
        return
    moments = refs[0]
    outs = refs[1:]
    learning = rate[0]
    for p in range(2):
        grad = total[p * rows : (p + 1) * rows] * scale
        first_new = 0.9 * moments[p].astype(jnp.float32) + 0.1 * grad
        second_new = 0.95 * moments[2 + p].astype(jnp.float32) + 0.05 * grad * grad
        update = learning * (first_new / bias_first) / (jnp.sqrt(second_new / bias_second) + 1e-08)
        outs[p][0] = (w_ref[p].astype(jnp.float32) - update).astype(jnp.bfloat16)
        outs[2 + p][0] = first_new.astype(jnp.bfloat16)
        outs[4 + p][0] = second_new.astype(jnp.bfloat16)


def step(blocks, ids, rate, weights, cot, total, moments, scale):
    count = len(blocks) // 2
    hidden, width = weights.shape[1], weights.shape[2]
    rows = hidden // halves
    first, last = total is None, moments is not None
    tokens = blocks[0].shape[0]

    def cot_map(k, i, ids, rate):
        return (ids[k], i, 0)

    def rows_map(i, ids, rate):
        return (0, i, 0)

    in_specs = [pl.BlockSpec((2, rows, width), rows_map)]
    in_specs += [pl.BlockSpec((tokens, width), lambda i, ids, rate: (0, 0))] * (2 * count)
    in_specs += [
        pl.BlockSpec((1, rows, cot.shape[2]), functools.partial(cot_map, k))
        for k in range(4 * count)
    ]
    args = [weights, *blocks, *([cot] * (4 * count))]
    if not first:
        in_specs.append(pl.BlockSpec((2, rows, width), rows_map))
        args.append(total)
    if last:
        in_specs.append(pl.BlockSpec((4, rows, width), rows_map))
        args.append(moments)
        out_shape = [jax.ShapeDtypeStruct((1, hidden, width), jnp.bfloat16)] * 6
        out_specs = [pl.BlockSpec((1, rows, width), rows_map)] * 6
    else:
        out_shape = jax.ShapeDtypeStruct((2, hidden, width), jnp.float32)
        out_specs = pl.BlockSpec((2, rows, width), rows_map)
    flops = 2 * 2 * (2 * hidden) * width * tokens * 2 * count
    return pl.pallas_call(
        functools.partial(step_kernel, count, first, last, scale),
        grid_spec=pltpu.PrefetchScalarGridSpec(
            num_scalar_prefetch=2, grid=(halves,), in_specs=in_specs, out_specs=out_specs
        ),
        out_shape=out_shape,
        compiler_params=pltpu.CompilerParams(vmem_limit_bytes=48 * 2**20),
        cost_estimate=pl.CostEstimate(
            flops=flops, bytes_accessed=10 * 2**20, transcendentals=hidden * tokens * 2 * count
        ),
    )(ids, rate, *args)


def pick_kernel(winner, held_ref, out_ref):
    out_ref[...] = held_ref[...]


def pick(held, winner):
    shape = held.shape
    return pl.pallas_call(
        pick_kernel,
        grid_spec=pltpu.PrefetchScalarGridSpec(
            num_scalar_prefetch=1,
            grid=(shape[0],),
            in_specs=[pl.BlockSpec((1,) + shape[1:], lambda i, winner: (winner[i], 0, 0))],
            out_specs=pl.BlockSpec((1,) + shape[1:], lambda i, winner: (i, 0, 0)),
        ),
        out_shape=jax.ShapeDtypeStruct(shape, held.dtype),
        cost_estimate=pl.CostEstimate(
            flops=0, bytes_accessed=4 * held.size, transcendentals=0
        ),
    )(winner, held)


def copy_winner(arrays, winner):
    members = lax.axis_size("member")
    whole = jnp.concatenate(arrays, axis=0)
    count, rows, width = whole.shape
    pieces = whole.reshape(members, count * rows // members, width)
    held = lax.all_to_all(pieces, "member", 0, 0, tiled=True)
    returned = lax.all_to_all(pick(held, winner), "member", 0, 0, tiled=True)
    return returned.reshape(count, rows, width)


def body(
    tokens,
    cotangent,
    gate_weight,
    up_weight,
    gate_first,
    up_first,
    gate_second,
    up_second,
    winner,
    rate_index,
):
    own = tokens[0]
    scale = own.shape[1] ** (-0.5)
    me = lax.axis_index("fsdp")
    z, low, core = me // 4, (me // 2) % 2, me % 2
    with jax.named_scope("gather"):
        block = jnp.concatenate([own, lax.ppermute(own, "fsdp", low_swap)], axis=0)
        up, down = block, block
        chunks = [(0, block)]
        for hop in range(1, 5):
            if hop < 4:
                up = lax.ppermute(up, "fsdp", z_up)
                chunks.append((-hop, up))
            down = lax.ppermute(down, "fsdp", z_down)
            chunks.append((hop, down))
        partners = [lax.ppermute(c, "fsdp", core_swap) for _, c in chunks]
    with jax.named_scope("cotangent"):
        turned = cotangent[0].T.reshape(32, cotangent.shape[2] // 32, cotangent.shape[1])
        cot = lax.all_to_all(turned, "fsdp", 0, 0, tiled=True)
    with jax.named_scope("weights"):
        weights = copy_winner([gate_weight, up_weight], winner)
    with jax.named_scope("moments"):
        moments = copy_winner([gate_first, up_first, gate_second, up_second], winner)
    learning = 0.2 * jnp.exp2(
        (rate_index[lax.axis_index("member")].astype(jnp.float32) - 2.0) * 0.5
    )
    rate = jnp.full((1,), learning, jnp.float32)

    def sources(offset):
        at = (z + offset + nz) % nz
        return [
            device(at, low, core),
            device(at, 1 - low, core),
            device(at, low, 1 - core),
            device(at, 1 - low, 1 - core),
        ]

    total = None
    groups = [[0], [1, 2], [3, 4], [5, 6], [7]]
    for number, group in enumerate(groups):
        blocks, ids = [], []
        for g in group:
            blocks += [chunks[g][1], partners[g]]
            ids += sources(chunks[g][0])
        last = number == len(groups) - 1
        with jax.named_scope("terms"):
            total = step(
                blocks,
                jnp.stack(ids).astype(jnp.int32),
                rate,
                weights,
                cot,
                total,
                moments if last else None,
                scale,
            )
    return tuple(total)


def solution(mesh):
    spread = P("member", "fsdp", None)
    return jax.shard_map(
        body,
        mesh=mesh,
        in_specs=(spread,) * 8 + (P(), P()),
        out_specs=(spread,) * 6,
        check_vma=False,
    )
```

```python
import functools

import jax
import jax.numpy as jnp
from jax import lax
from jax.experimental import pallas as pl
from jax.experimental.pallas import tpu as pltpu
from jax.sharding import PartitionSpec as P

gelu_c = 0.7978845608028654
bias_first = 1.0 - 0.9**10
bias_second = 1.0 - 0.95**10
nz = 8
halves = 2


def device(z, low, core):
    return (z * 2 + low) * 2 + core


everyone = [(z, low, core) for z in range(nz) for low in range(2) for core in range(2)]
z_up = [(device(z, a, c), device((z + 1) % nz, a, c)) for z, a, c in everyone]
z_down = [(b, a) for a, b in z_up]
core_swap = [(i, i ^ 1) for i in range(32)]
same_core = [[i for i in range(32) if i % 2 == core] for core in range(2)]
low_swap = [(i, i ^ 2) for i in range(32)]
row_swap = [(m, m ^ 1) for m in range(8)]


def along_row(hops):
    return [(m, (m + 2 * hops) % 8) for m in range(8)]


def gelu_parts(gate_pre):
    tangent = jnp.tanh(gelu_c * (gate_pre + 0.044715 * gate_pre * gate_pre * gate_pre))
    activated = 0.5 * gate_pre * (1.0 + tangent)
    slope = 0.5 * (1.0 + tangent) + 0.5 * gate_pre * (1.0 - tangent * tangent) * gelu_c * (
        1.0 + 3.0 * 0.044715 * gate_pre * gate_pre
    )
    return (activated, slope)


def block_terms(weights, token_block, cot, scale):
    half = cot.shape[0]
    pre = (
        lax.dot_general(
            weights, token_block, (((1,), (1,)), ((), ())), preferred_element_type=jnp.float32
        )
        * scale
    )
    activated, slope = gelu_parts(pre[:half])
    gate_cot = (cot * pre[half:] * slope).astype(jnp.bfloat16)
    up_cot = (cot * activated).astype(jnp.bfloat16)
    return jnp.dot(
        jnp.concatenate([gate_cot, up_cot], axis=0),
        token_block,
        preferred_element_type=jnp.float32,
    )


def step_kernel(count, first, scale, ids, w_ref, *refs):
    tokens = refs[:count]
    cots = refs[count : 3 * count]
    rows, width = w_ref.shape[1], w_ref.shape[2]
    weights = w_ref[...].reshape(2 * rows, width)
    total = None if first else refs[3 * count][...].reshape(2 * rows, width)
    for j in range(count):
        cot = jnp.concatenate([cots[2 * j][0], cots[2 * j + 1][0]], axis=1).astype(jnp.float32)
        part = block_terms(weights, tokens[j][...], cot, scale)
        total = part if total is None else total + part
    refs[-1][...] = total.reshape(2, rows, width)


def step(blocks, ids, weights, cot, total, scale):
    count = len(blocks)
    hidden, width = weights.shape[1], weights.shape[2]
    rows = hidden // halves
    first = total is None
    tokens = blocks[0].shape[0]

    def cot_map(k, i, ids):
        return (ids[k], i, 0)

    def rows_map(i, ids):
        return (0, i, 0)

    in_specs = [pl.BlockSpec((2, rows, width), rows_map)]
    in_specs += [pl.BlockSpec((tokens, width), lambda i, ids: (0, 0))] * count
    in_specs += [
        pl.BlockSpec((1, rows, cot.shape[2]), functools.partial(cot_map, k))
        for k in range(2 * count)
    ]
    args = [weights, *blocks, *([cot] * (2 * count))]
    if not first:
        in_specs.append(pl.BlockSpec((2, rows, width), rows_map))
        args.append(total)
    return pl.pallas_call(
        functools.partial(step_kernel, count, first, scale),
        grid_spec=pltpu.PrefetchScalarGridSpec(
            num_scalar_prefetch=1,
            grid=(halves,),
            in_specs=in_specs,
            out_specs=pl.BlockSpec((2, rows, width), rows_map),
        ),
        out_shape=jax.ShapeDtypeStruct((2, hidden, width), jnp.float32),
        compiler_params=pltpu.CompilerParams(vmem_limit_bytes=48 * 2**20),
        cost_estimate=pl.CostEstimate(
            flops=8 * hidden * width * tokens * count,
            bytes_accessed=8 * 2**20,
            transcendentals=hidden * tokens * count,
        ),
    )(ids, *args)


def adam_kernel(scale, rate, w_ref, first_ref, second_ref, mine_ref, other_ref, *outs):
    learning = rate[0]
    for p in range(2):
        grad = (mine_ref[p] + other_ref[p]) * scale
        first_new = 0.9 * first_ref[p].astype(jnp.float32) + 0.1 * grad
        second_new = 0.95 * second_ref[p].astype(jnp.float32) + 0.05 * grad * grad
        update = learning * (first_new / bias_first) / (jnp.sqrt(second_new / bias_second) + 1e-08)
        outs[p][0] = (w_ref[p].astype(jnp.float32) - update).astype(jnp.bfloat16)
        outs[2 + p][0] = first_new.astype(jnp.bfloat16)
        outs[4 + p][0] = second_new.astype(jnp.bfloat16)


def adam(weights, firsts, seconds, mine, other, rate, scale):
    hidden, width = weights.shape[1], weights.shape[2]
    rows = 32
    pair = pl.BlockSpec((2, rows, width), lambda i, rate: (0, i, 0))
    one = pl.BlockSpec((1, rows, width), lambda i, rate: (0, i, 0))
    return pl.pallas_call(
        functools.partial(adam_kernel, scale),
        grid_spec=pltpu.PrefetchScalarGridSpec(
            num_scalar_prefetch=1, grid=(hidden // rows,), in_specs=[pair] * 5, out_specs=[one] * 6
        ),
        out_shape=[jax.ShapeDtypeStruct((1, hidden, width), jnp.bfloat16)] * 6,
        compiler_params=pltpu.CompilerParams(vmem_limit_bytes=48 * 2**20),
    )(rate, weights, firsts, seconds, mine, other)


def pick_kernel(sources, index, *refs):
    outs = refs[sources:]
    for k in range(index.shape[0]):
        for i in range(sources):

            @pl.when(index[k] == i)
            def _():
                target = outs[k] if len(outs) > 1 else outs[0].at[k]
                target[...] = refs[i][...]


def pick(arrays, index, together):
    shape, count = arrays[0].shape, index.shape[0]
    kind = arrays[0].dtype
    whole = pl.BlockSpec(memory_space=pltpu.VMEM)
    if together:
        out_shape = jax.ShapeDtypeStruct((count,) + shape, kind)
        out_specs = whole
    else:
        out_shape = [jax.ShapeDtypeStruct(shape, kind)] * count
        out_specs = [whole] * count
    return pl.pallas_call(
        functools.partial(pick_kernel, len(arrays)),
        in_specs=[pl.BlockSpec(memory_space=pltpu.SMEM)] + [whole] * len(arrays),
        out_specs=out_specs,
        out_shape=out_shape,
        compiler_params=pltpu.CompilerParams(vmem_limit_bytes=32 * 2**20),
    )(index, *arrays)


def in_pieces(first, second):
    rows = first.shape[1] // 2
    return [first[0, :rows], first[0, rows:], second[0, :rows], second[0, rows:]]


def spread(pieces):
    return [lax.ppermute(pieces[j], "member", along_row(j)) for j in (1, 2, 3)]


def routes(winner):
    me = lax.axis_index("member").astype(jnp.int32)
    column, row = me // 2, me % 2
    order = jnp.arange(8, dtype=jnp.int32)
    losing = winner != order
    low = jnp.min(jnp.where(losing, order, 8))
    high = jnp.max(jnp.where(losing, order, -1))

    def won(m):
        return jnp.sum(jnp.where(order == m, winner, 0))

    cross = jnp.stack([(column - won(m) // 2 + 4) % 4 for m in (low, high)])
    gather = []
    for j in range(4):
        target = ((column + j) % 4) * 2 + row
        source = won(target)
        here = (column - source // 2 + 4) % 4
        there = jnp.where(target == low, 4, 5)
        gather.append(jnp.where(source % 2 == row, here, there))
    mine = won(me)
    place = jnp.stack([(column - mine // 2 - p + 8) % 4 for p in range(4)])
    return cross.astype(jnp.int32), jnp.stack(gather).astype(jnp.int32), place.astype(jnp.int32)


def body(
    tokens,
    cotangent,
    gate_weight,
    up_weight,
    gate_first,
    up_first,
    gate_second,
    up_second,
    winner,
    rate_index,
):
    sync = lax.optimization_barrier
    own = tokens[0]
    count, width = own.shape
    hidden = gate_weight.shape[1]
    scale = width ** (-0.5)
    me = lax.axis_index("fsdp").astype(jnp.int32)
    z, low, core = me // 4, (me // 2) % 2, me % 2
    cross, gather, place = routes(winner)
    learning = 0.2 * jnp.exp2(
        (rate_index[lax.axis_index("member")].astype(jnp.float32) - 2.0) * 0.5
    )
    rate = jnp.full((1,), learning, jnp.float32)

    def fsdp(value, pairs):
        return lax.ppermute(value, "fsdp", pairs)

    def exchange(held):
        return lax.ppermute(pick(held, cross, True), "member", row_swap)

    def gathered(held, came):
        sent = pick([*held, came[0], came[1]], gather, False)
        return [sent[0], *spread(sent)]

    def settled(got):
        return pick(got, place, True).reshape(2, hidden, width)

    def ids(half, *sources):
        side = core if half == 0 else 1 - core
        return jnp.stack(
            [(((z + d + nz) % nz) * 2 + (low + b) % 2) * 2 + side for d, b in sources]
        ).astype(jnp.int32)

    bundles = [
        in_pieces(gate_weight, up_weight),
        in_pieces(gate_first, up_first),
        in_pieces(gate_second, up_second),
    ]
    turned = cotangent[0].T.reshape(16, 2 * hidden, count)
    with jax.named_scope("tick_a"):
        turned = lax.all_to_all(
            turned, "fsdp", 0, 0, axis_index_groups=same_core, tiled=True
        )
        partner = fsdp(own, low_swap)
        up, down = fsdp(own, z_up), fsdp(own, z_down)
        held0 = [bundles[0][0], *spread(bundles[0])]
    partner, up1, down1, held0 = sync((partner, up, down, held0))
    with jax.named_scope("tick_b"):
        up2 = fsdp(jnp.concatenate([up1, partner]), z_up)
        down2 = fsdp(jnp.concatenate([down1, partner]), z_down)
        came0 = exchange(held0)
        held1 = [bundles[1][0], *spread(bundles[1])]
    up2, down2, came0, held1, held0, bundles[2] = sync(
        (up2, down2, came0, held1, held0, bundles[2])
    )
    with jax.named_scope("tick_c"):
        up3, down3 = fsdp(up2, z_up), fsdp(down2, z_down)
        got0 = gathered(held0, came0)
    up3, down3, got0, held1, bundles[2] = sync((up3, down3, got0, held1, bundles[2]))
    with jax.named_scope("tick_d"):
        mine = settled(got0)
        theirs = fsdp(mine, core_swap)
        up4, down4 = fsdp(up3[count:], z_up), fsdp(down3, z_down)
        came1 = exchange(held1)
        held2 = [bundles[2][0], *spread(bundles[2])]
        cot = turned.reshape(32, hidden, count)
        blocks = [
            jnp.concatenate([own, partner]),
            jnp.concatenate([up1, down1]),
            up2,
            down2,
        ]
        sources = [(0, 0), (0, 1), (-1, 0), (1, 0), (-2, 0), (-1, 1), (2, 0), (1, 1)]
        total = [
            step(blocks, ids(half, *sources), w, cot, None, scale)
            for half, w in ((0, mine), (1, theirs))
        ]
    up4, down4, came1, held2, total, held1 = sync((up4, down4, came1, held2, total, held1))
    with jax.named_scope("tick_e"):
        last = fsdp(down4[count:], z_down)
        got1 = gathered(held1, came1)
        came2 = exchange(held2)
        sources = [(-3, 0), (-2, 1), (3, 0), (2, 1), (4, 0), (3, 1)]
        total = [
            step([up3, down3, down4], ids(half, *sources), w, cot, t, scale)
            for half, w, t in ((0, mine, total[0]), (1, theirs, total[1]))
        ]
    last, got1, came2, total, held2 = sync((last, got1, came2, total, held2))
    with jax.named_scope("tick_f"):
        got2 = gathered(held2, came2)
        firsts = settled(got1)
        blocks = [jnp.concatenate([up4, last])]
        sources = [(-3, 1), (4, 1)]
        send = step(blocks, ids(1, *sources), theirs, cot, total[1], scale)
        other = fsdp(send, core_swap)
        keep = step(blocks, ids(0, *sources), mine, cot, total[0], scale)
    with jax.named_scope("adam"):
        seconds = settled(got2)
        return tuple(adam(mine, firsts, seconds, keep, other, rate, scale))


def solution(mesh):
    split = P("member", "fsdp", None)
    return jax.shard_map(
        body,
        mesh=mesh,
        in_specs=(split,) * 8 + (P(), P()),
        out_specs=(split,) * 6,
        check_vma=False,
    )
```

```python
import functools

import jax
import jax.numpy as jnp
from jax import lax
from jax.experimental import pallas as pl
from jax.experimental.pallas import tpu as pltpu
from jax.sharding import PartitionSpec as P

gelu_c = 0.7978845608028654
bias_first = 1.0 - 0.9**10
bias_second = 1.0 - 0.95**10
nz = 8
tile = 256


def device(z, low, core):
    return (z * 2 + low) * 2 + core


everyone = [(z, low, core) for z in range(nz) for low in range(2) for core in range(2)]
z_up = [(device(z, a, c), device((z + 1) % nz, a, c)) for z, a, c in everyone]
z_down = [(b, a) for a, b in z_up]
core_swap = [(i, i ^ 1) for i in range(32)]
same_core = [[i for i in range(32) if i % 2 == core] for core in range(2)]
low_swap = [(i, i ^ 2) for i in range(32)]
row_swap = [(m, m ^ 1) for m in range(8)]


rows_of_members = [[m for m in range(8) if m % 2 == row] for row in range(2)]


def along_row(hops):
    return [(m, (m + 2 * hops) % 8) for m in range(8)]


def gelu_parts(gate_pre):
    tangent = jnp.tanh(gelu_c * (gate_pre + 0.044715 * gate_pre * gate_pre * gate_pre))
    activated = 0.5 * gate_pre * (1.0 + tangent)
    slope = 0.5 * (1.0 + tangent) + 0.5 * gate_pre * (1.0 - tangent * tangent) * gelu_c * (
        1.0 + 3.0 * 0.044715 * gate_pre * gate_pre
    )
    return (activated, slope)


def launch(copies):
    for copy in copies:
        copy.start()
    for copy in copies:
        copy.wait()


def terms_kernel(lengths, sources, first, scale, here, mine, theirs, cots, *refs):
    count = len(lengths)
    tokens, refs = refs[:count], refs[count:]
    if not first:
        kept, sent, refs = refs[:2], refs[2:4], refs[4:]
    keep, send = refs[:2], refs[2:4]
    x, c, w, grad, cot, sems = refs[4:]
    rows, hidden = mine.shape[1], 2 * mine.shape[1]
    me = here[1]
    z, low, core = me // 4, (me // 2) % 2, me % 2
    mine_at = pl.multiple_of(core * rows, 32)
    theirs_at = pl.multiple_of((1 - core) * rows, 32)
    pairs = []
    for p in range(2):
        pairs.append((mine.at[p], w.at[pl.ds(p * hidden + mine_at, rows)]))
        pairs.append((theirs.at[p], w.at[pl.ds(p * hidden + theirs_at, rows)]))
    at = 0
    for ref, length in zip(tokens, lengths):
        pairs.append((ref, x.at[pl.ds(at, length)]))
        at += length
    for k, (hops, other) in enumerate(sources):
        source = ((z + hops + nz) % nz) * 2 + (low + other) % 2
        pairs.append((cots.at[source], c.at[k]))
    ready = len(pairs)
    if not first:
        for p in range(2):
            pairs.append((kept[p], grad.at[pl.ds(p * hidden + mine_at, rows)]))
            pairs.append((sent[p], grad.at[pl.ds(p * hidden + theirs_at, rows)]))
    copies = [pltpu.make_async_copy(a, b, sems.at[k]) for k, (a, b) in enumerate(pairs)]
    for copy in copies:
        copy.start()
    for copy in copies[:ready]:
        copy.wait()

    @pl.loop(0, x.shape[0] // tile)
    def _(t):
        block = x[pl.ds(pl.multiple_of(t * tile, tile), tile), :]
        pre = (
            lax.dot_general(
                w[...], block, (((1,), (1,)), ((), ())), preferred_element_type=jnp.float32
            )
            * scale
        )
        value = jnp.concatenate([c[2 * t], c[2 * t + 1]], axis=1).astype(jnp.float32)
        activated, slope = gelu_parts(pre[:hidden])
        columns = pl.ds(pl.multiple_of(t * tile, tile), tile)
        cot[pl.ds(0, hidden), columns] = (value * pre[hidden:] * slope).astype(jnp.bfloat16)
        cot[pl.ds(hidden, hidden), columns] = (value * activated).astype(jnp.bfloat16)

    for copy in copies[ready:]:
        copy.wait()

    @pl.loop(0, x.shape[1] // tile)
    def _(n):
        columns = pl.ds(pl.multiple_of(n * tile, tile), tile)
        part = jnp.dot(cot[...], x[:, columns], preferred_element_type=jnp.float32)
        if first:
            grad[:, columns] = part
        else:
            grad[:, columns] += part

    outs = []
    for p in range(2):
        outs.append((grad.at[pl.ds(p * hidden + theirs_at, rows)], send[p]))
        outs.append((grad.at[pl.ds(p * hidden + mine_at, rows)], keep[p]))
    launch([pltpu.make_async_copy(a, b, sems.at[k]) for k, (a, b) in enumerate(outs)])


def terms(here, mine, theirs, cots, blocks, sources, totals, scale):
    rows, width = mine.shape[1], mine.shape[2]
    total = sum(b.shape[0] for b in blocks)
    first = totals is None
    anywhere = pl.BlockSpec(memory_space=pl.ANY)
    args = [mine, theirs, cots, *blocks, *([] if first else totals)]
    sums = jax.ShapeDtypeStruct((rows, width), jnp.float32)
    kernel = functools.partial(
        terms_kernel, tuple(b.shape[0] for b in blocks), tuple(sources), first, scale
    )
    return pl.pallas_call(
        kernel,
        in_specs=[pl.BlockSpec(memory_space=pltpu.SMEM)] + [anywhere] * len(args),
        out_specs=[anywhere] * 4,
        out_shape=[sums] * 4,
        scratch_shapes=[
            pltpu.VMEM((total, width), jnp.bfloat16),
            pltpu.VMEM((len(sources), 2 * rows, cots.shape[2]), jnp.bfloat16),
            pltpu.VMEM((4 * rows, width), jnp.bfloat16),
            pltpu.VMEM((4 * rows, width), jnp.float32),
            pltpu.VMEM((4 * rows, total), jnp.bfloat16),
            pltpu.SemaphoreType.DMA((8 + len(blocks) + len(sources),)),
        ],
        compiler_params=pltpu.CompilerParams(vmem_limit_bytes=48 * 2**20),
        cost_estimate=pl.CostEstimate(
            flops=16 * rows * width * total,
            bytes_accessed=20 * 2**20,
            transcendentals=2 * rows * total,
        ),
    )(here, *args)


def moved(here, winner, part):
    source = winner[here[0]]
    return (here[0] // 2 - source // 2 - part + 8) % 4


def adam_kernel(scale, here, winner, rate, w_ref, *refs):
    got, kept, came, outs = refs[0], refs[1:3], refs[3:5], refs[5:]
    learning = rate[0]
    column = winner[here[0]] // 2

    def moment(part):
        return got[(column + part) % 4].astype(jnp.float32)

    for p in range(2):
        grad = (kept[p][...] + came[p][...]) * scale
        first_new = 0.9 * moment(p) + 0.1 * grad
        second_new = 0.95 * moment(2 + p) + 0.05 * grad * grad
        update = learning * (first_new / bias_first) / (jnp.sqrt(second_new / bias_second) + 1e-08)
        outs[p][0] = (w_ref[p].astype(jnp.float32) - update).astype(jnp.bfloat16)
        outs[2 + p][0] = first_new.astype(jnp.bfloat16)
        outs[4 + p][0] = second_new.astype(jnp.bfloat16)


def adam(here, winner, rate, weights, got, mine, other, scale):
    hidden, width = weights.shape[1], weights.shape[2]
    rows = 32
    pair = pl.BlockSpec((2, rows, width), lambda i, *_: (0, i, 0))
    four = pl.BlockSpec((4, rows, width), lambda i, *_: (0, i, 0))
    flat = pl.BlockSpec((rows, width), lambda i, *_: (i, 0))
    one = pl.BlockSpec((1, rows, width), lambda i, *_: (0, i, 0))
    return pl.pallas_call(
        functools.partial(adam_kernel, scale),
        grid_spec=pltpu.PrefetchScalarGridSpec(
            num_scalar_prefetch=3,
            grid=(hidden // rows,),
            in_specs=[pair, four] + [flat] * 4,
            out_specs=[one] * 6,
        ),
        out_shape=[jax.ShapeDtypeStruct((1, hidden, width), jnp.bfloat16)] * 6,
        compiler_params=pltpu.CompilerParams(vmem_limit_bytes=48 * 2**20),
    )(here, winner, rate, weights, got, *mine, *other)


def losers(winner):
    low, high = 0, 0
    for m in range(7, -1, -1):
        low = jnp.where(winner[m] != m, m, low)
    for m in range(8):
        high = jnp.where(winner[m] != m, m, high)
    return low, high


def route(mode, here, winner):
    member = here[0]
    column, row = member // 2, member % 2
    low, high = losers(winner)
    if mode == "cross":
        return [(column - winner[m] // 2 + 4) % 4 for m in (low, high)]
    if mode == "place":
        return [moved(here, winner, part) for part in range(4)]
    wanted = []
    for j in range(4):
        target = j * 2 + row if mode == "columns" else ((column + j) % 4) * 2 + row
        source = winner[target]
        inside = (column - source // 2 + 4) % 4
        outside = jnp.where(target == low, 4, 5)
        wanted.append(jnp.where(source % 2 == row, inside, outside))
    return wanted


def pick_kernel(mode, here, winner, *refs):
    count = 2 if mode == "cross" else 4
    sems = refs[-1]
    if mode == "gather":
        outs, refs = list(refs[-5:-1]), list(refs[:-5])
    else:
        outs, refs = [refs[-2].at[k] for k in range(count)], list(refs[:-2])
    if mode in ("gather", "columns"):
        came = refs.pop()
        refs += [came.at[0], came.at[1]]
    index = route(mode, here, winner)
    for k in range(count):
        for i, ref in enumerate(refs):

            @pl.when(index[k] == i)
            def _():
                pltpu.make_async_copy(ref, outs[k], sems.at[k]).start()

    for k in range(count):
        pltpu.make_async_copy(refs[0], outs[k], sems.at[k]).wait()


def pick(mode, here, winner, arrays):
    shape, kind = arrays[0].shape, arrays[0].dtype
    smem = pl.BlockSpec(memory_space=pltpu.SMEM)
    anywhere = pl.BlockSpec(memory_space=pl.ANY)
    if mode == "gather":
        out_shape, out_specs = [jax.ShapeDtypeStruct(shape, kind)] * 4, [anywhere] * 4
    else:
        count = 2 if mode == "cross" else 4
        out_shape, out_specs = jax.ShapeDtypeStruct((count,) + shape, kind), anywhere
    return pl.pallas_call(
        functools.partial(pick_kernel, mode),
        in_specs=[smem, smem] + [anywhere] * len(arrays),
        out_specs=out_specs,
        out_shape=out_shape,
        scratch_shapes=[pltpu.SemaphoreType.DMA((4,))],
    )(here, winner, *arrays)


def spread(pieces):
    return [lax.ppermute(pieces[j], "member", along_row(j)) for j in (1, 2, 3)]


def body(
    tokens,
    cotangent,
    gate_weight,
    up_weight,
    gate_first,
    up_first,
    gate_second,
    up_second,
    winner,
    rate_index,
):
    sync = lax.optimization_barrier
    own = tokens[0]
    count, width = own.shape
    hidden = gate_weight.shape[1]
    scale = width ** (-0.5)
    here = jnp.stack([lax.axis_index("member"), lax.axis_index("fsdp")]).astype(jnp.int32)
    learning = 0.2 * jnp.exp2(
        (rate_index[lax.axis_index("member")].astype(jnp.float32) - 2.0) * 0.5
    )
    rate = jnp.full((1,), learning, jnp.float32)

    def fsdp(value, pairs):
        return lax.ppermute(value, "fsdp", pairs)

    def exchange(held):
        return lax.ppermute(pick("cross", here, winner, held), "member", row_swap)

    def gathered(held, came):
        sent = pick("gather", here, winner, [*held, came])
        return [sent[0], *spread(sent)]

    half = hidden // 2
    weights = [w[0, k * half : (k + 1) * half] for w in (gate_weight, up_weight) for k in range(2)]
    moments = [m[0] for m in (gate_first, up_first, gate_second, up_second)]
    turned = cotangent[0].T.reshape(16, 2 * hidden, count)
    with jax.named_scope("tick_a"):
        cots = lax.all_to_all(turned, "fsdp", 0, 0, axis_index_groups=same_core, tiled=True)
        start = jnp.concatenate([own, fsdp(own, low_swap)])
        held0 = [weights[0], *spread(weights)]
    start, held0, moments = sync((start, held0, moments))
    with jax.named_scope("tick_b"):
        up1, down1 = fsdp(start, z_up), fsdp(start, z_down)
        came0 = exchange(held0)
        held1 = [moments[0], *spread(moments)]
    up1, down1, came0, held0, cots = sync((up1, down1, came0, held0, cots))
    with jax.named_scope("tick_c"):
        up2, down2 = fsdp(up1, z_up), fsdp(down1, z_down)
        got0 = gathered(held0, came0)
    up2, down2, got0, held1 = sync((up2, down2, got0, held1))
    with jax.named_scope("tick_d"):
        up3, down3 = fsdp(up2, z_up), fsdp(down2, z_down)
        came1 = exchange(held1)
        mine = pick("place", here, winner, got0).reshape(2, hidden, width)
        theirs = fsdp(mine, core_swap)
        blocks = [start, up1, down1, up2, down2]
        sources = [(d, b) for d in (0, -1, 1, -2, 2) for b in range(2)]
        totals = terms(here, mine, theirs, cots, blocks, sources, None, scale)
    up3, down3, came1, totals, held1 = sync((up3, down3, came1, totals, held1))
    with jax.named_scope("tick_e"):
        sides = [fsdp(up3[:count], z_up), fsdp(down3[count:], z_down)]
        got1 = lax.all_to_all(
            pick("columns", here, winner, [*held1, came1]),
            "member",
            0,
            0,
            axis_index_groups=rows_of_members,
            tiled=True,
        )
        sources = [(d, b) for d in (-3, 3, 4) for b in range(2)]
        sums = terms(here, mine, theirs, cots, [up3, down3, *sides], sources, totals, scale)
        other = [fsdp(part, core_swap) for part in sums[2:]]
    with jax.named_scope("adam"):
        return tuple(adam(here, winner, rate, mine, got1, sums[:2], other, scale))


def solution(mesh):
    split = P("member", "fsdp", None)
    return jax.shard_map(
        body,
        mesh=mesh,
        in_specs=(split,) * 8 + (P(), P()),
        out_specs=(split,) * 6,
        check_vma=False,
    )
```

```python
import functools

import jax
import jax.numpy as jnp
from jax import lax
from jax.experimental import pallas as pl
from jax.experimental.pallas import tpu as pltpu
from jax.sharding import PartitionSpec as P

gelu_c = 0.7978845608028654
bias_first = 1.0 - 0.9**10
bias_second = 1.0 - 0.95**10
nz = 8
tile = 256


def device(z, low, core):
    return (z * 2 + low) * 2 + core


everyone = [(z, low, core) for z in range(nz) for low in range(2) for core in range(2)]
z_up = [(device(z, a, c), device((z + 1) % nz, a, c)) for z, a, c in everyone]
z_down = [(b, a) for a, b in z_up]
core_swap = [(i, i ^ 1) for i in range(32)]
same_core = [[i for i in range(32) if i % 2 == core] for core in range(2)]
low_swap = [(i, i ^ 2) for i in range(32)]
row_swap = [(m, m ^ 1) for m in range(8)]


rows_of_members = [[m for m in range(8) if m % 2 == row] for row in range(2)]


def along_row(hops):
    return [(m, (m + 2 * hops) % 8) for m in range(8)]


def gelu_parts(gate_pre):
    tangent = jnp.tanh(gelu_c * (gate_pre + 0.044715 * gate_pre * gate_pre * gate_pre))
    activated = 0.5 * gate_pre * (1.0 + tangent)
    slope = 0.5 * (1.0 + tangent) + 0.5 * gate_pre * (1.0 - tangent * tangent) * gelu_c * (
        1.0 + 3.0 * 0.044715 * gate_pre * gate_pre
    )
    return (activated, slope)


def launch(copies):
    for copy in copies:
        copy.start()
    for copy in copies:
        copy.wait()


def terms_kernel(lengths, sources, first, scale, here, mine, theirs, cots, *refs):
    count = len(lengths)
    tokens, refs = refs[:count], refs[count:]
    if not first:
        kept, sent, refs = refs[:2], refs[2:6], refs[6:]
    keep, send = refs[:2], refs[2:6]
    x, c, w, grad, cot, sems = refs[6:]
    rows, hidden = mine.shape[1], 2 * mine.shape[1]
    half = rows // 2
    me = here[1]
    z, low, core = me // 4, (me // 2) % 2, me % 2
    mine_at = pl.multiple_of(core * rows, 32)
    theirs_at = pl.multiple_of((1 - core) * rows, 32)
    pairs = []
    for p in range(2):
        pairs.append((mine.at[p], w.at[pl.ds(p * hidden + mine_at, rows)]))
        pairs.append((theirs.at[p], w.at[pl.ds(p * hidden + theirs_at, rows)]))
    at = 0
    for ref, length in zip(tokens, lengths):
        pairs.append((ref, x.at[pl.ds(at, length)]))
        at += length
    for k, (hops, other) in enumerate(sources):
        source = ((z + hops + nz) % nz) * 2 + (low + other) % 2
        pairs.append((cots.at[source], c.at[k]))
    ready = len(pairs)
    if not first:
        for p in range(2):
            pairs.append((kept[p], grad.at[pl.ds(p * hidden + mine_at, rows)]))
            for h in range(2):
                to = p * hidden + theirs_at + h * half
                pairs.append((sent[2 * p + h], grad.at[pl.ds(to, half)]))
    copies = [pltpu.make_async_copy(a, b, sems.at[k]) for k, (a, b) in enumerate(pairs)]
    for copy in copies:
        copy.start()
    for copy in copies[:ready]:
        copy.wait()

    @pl.loop(0, x.shape[0] // tile)
    def _(t):
        block = x[pl.ds(pl.multiple_of(t * tile, tile), tile), :]
        pre = (
            lax.dot_general(
                w[...], block, (((1,), (1,)), ((), ())), preferred_element_type=jnp.float32
            )
            * scale
        )
        value = jnp.concatenate([c[2 * t], c[2 * t + 1]], axis=1).astype(jnp.float32)
        activated, slope = gelu_parts(pre[:hidden])
        columns = pl.ds(pl.multiple_of(t * tile, tile), tile)
        cot[pl.ds(0, hidden), columns] = (value * pre[hidden:] * slope).astype(jnp.bfloat16)
        cot[pl.ds(hidden, hidden), columns] = (value * activated).astype(jnp.bfloat16)

    for copy in copies[ready:]:
        copy.wait()

    @pl.loop(0, x.shape[1] // tile)
    def _(n):
        columns = pl.ds(pl.multiple_of(n * tile, tile), tile)
        part = jnp.dot(cot[...], x[:, columns], preferred_element_type=jnp.float32)
        if first:
            grad[:, columns] = part
        else:
            grad[:, columns] += part

    outs = []
    for p in range(2):
        for h in range(2):
            to = p * hidden + theirs_at + h * half
            outs.append((grad.at[pl.ds(to, half)], send[2 * p + h]))
        outs.append((grad.at[pl.ds(p * hidden + mine_at, rows)], keep[p]))
    launch([pltpu.make_async_copy(a, b, sems.at[k]) for k, (a, b) in enumerate(outs)])


def terms(here, mine, theirs, cots, blocks, sources, totals, scale):
    rows, width = mine.shape[1], mine.shape[2]
    total = sum(b.shape[0] for b in blocks)
    first = totals is None
    anywhere = pl.BlockSpec(memory_space=pl.ANY)
    args = [mine, theirs, cots, *blocks, *([] if first else totals)]
    sums = jax.ShapeDtypeStruct((rows, width), jnp.float32)
    parts = jax.ShapeDtypeStruct((rows // 2, width), jnp.float32)
    kernel = functools.partial(
        terms_kernel, tuple(b.shape[0] for b in blocks), tuple(sources), first, scale
    )
    return pl.pallas_call(
        kernel,
        in_specs=[pl.BlockSpec(memory_space=pltpu.SMEM)] + [anywhere] * len(args),
        out_specs=[anywhere] * 6,
        out_shape=[sums] * 2 + [parts] * 4,
        scratch_shapes=[
            pltpu.VMEM((total, width), jnp.bfloat16),
            pltpu.VMEM((len(sources), 2 * rows, cots.shape[2]), jnp.bfloat16),
            pltpu.VMEM((4 * rows, width), jnp.bfloat16),
            pltpu.VMEM((4 * rows, width), jnp.float32),
            pltpu.VMEM((4 * rows, total), jnp.bfloat16),
            pltpu.SemaphoreType.DMA((10 + len(blocks) + len(sources),)),
        ],
        compiler_params=pltpu.CompilerParams(vmem_limit_bytes=48 * 2**20),
        cost_estimate=pl.CostEstimate(
            flops=16 * rows * width * total,
            bytes_accessed=20 * 2**20,
            transcendentals=2 * rows * total,
        ),
    )(here, *args)


def moved(here, winner, part):
    source = winner[here[0]]
    return (here[0] // 2 - source // 2 - part + 8) % 4


def adam_kernel(scale, here, winner, rate, w_ref, *refs):
    got, kept, came, outs = refs[0], refs[1:3], refs[3:5], refs[-6:]
    learning = rate[0]
    column = winner[here[0]] // 2

    def moment(part):
        return got[(column + part) % 4].astype(jnp.float32)

    for p in range(2):
        grad = (kept[p][...] + came[p][...]) * scale
        first_new = 0.9 * moment(p) + 0.1 * grad
        second_new = 0.95 * moment(2 + p) + 0.05 * grad * grad
        update = learning * (first_new / bias_first) / (jnp.sqrt(second_new / bias_second) + 1e-08)
        outs[p][0] = (w_ref[p].astype(jnp.float32) - update).astype(jnp.bfloat16)
        outs[2 + p][0] = first_new.astype(jnp.bfloat16)
        outs[4 + p][0] = second_new.astype(jnp.bfloat16)


def adam(here, winner, rate, weights, got, mine, other, scale, part, earlier):
    hidden, width = weights.shape[1], weights.shape[2]
    rows = 16
    steps = got.shape[1] // rows
    off = part * steps
    pair = pl.BlockSpec((2, rows, width), lambda i, *_: (0, i + off, 0))
    four = pl.BlockSpec((4, rows, width), lambda i, *_: (0, i, 0))
    flat = pl.BlockSpec((rows, width), lambda i, *_: (i + off, 0))
    piece = pl.BlockSpec((rows, width), lambda i, *_: (i, 0))
    one = pl.BlockSpec((1, rows, width), lambda i, *_: (0, i + off, 0))
    whole = pl.BlockSpec(memory_space=pl.ANY)
    return pl.pallas_call(
        functools.partial(adam_kernel, scale),
        grid_spec=pltpu.PrefetchScalarGridSpec(
            num_scalar_prefetch=3,
            grid=(steps,),
            in_specs=[pair, four] + [flat] * 2 + [piece] * 2 + [whole] * len(earlier),
            out_specs=[one] * 6,
        ),
        out_shape=[jax.ShapeDtypeStruct((1, hidden, width), jnp.bfloat16)] * 6,
        input_output_aliases={9 + k: k for k in range(len(earlier))},
        compiler_params=pltpu.CompilerParams(vmem_limit_bytes=32 * 2**20),
        cost_estimate=pl.CostEstimate(
            flops=40 * hidden * width, bytes_accessed=8 * 2**20, transcendentals=hidden * width
        ),
    )(here, winner, rate, weights, got, *mine, *other, *earlier)


def losers(winner):
    low, high = 0, 0
    for m in range(7, -1, -1):
        low = jnp.where(winner[m] != m, m, low)
    for m in range(8):
        high = jnp.where(winner[m] != m, m, high)
    return low, high


def route(mode, here, winner):
    member = here[0]
    column, row = member // 2, member % 2
    low, high = losers(winner)
    if mode == "cross":
        return [(column - winner[m] // 2 + 4) % 4 for m in (low, high)]
    if mode == "place":
        return [moved(here, winner, part) for part in range(4)]
    wanted = []
    for j in range(4):
        target = j * 2 + row if mode == "columns" else ((column + j) % 4) * 2 + row
        source = winner[target]
        inside = (column - source // 2 + 4) % 4
        outside = jnp.where(target == low, 4, 5)
        wanted.append(jnp.where(source % 2 == row, inside, outside))
    return wanted


def pick_kernel(mode, span, here, winner, *refs):
    count = 2 if mode == "cross" else 4
    stage, sems = refs[-2:]
    if mode == "gather":
        outs, refs = list(refs[-6:-2]), list(refs[:-6])
    else:
        outs, refs = [refs[-3].at[k] for k in range(count)], list(refs[:-3])
    came = []
    if mode in ("gather", "columns"):
        last = refs.pop()
        came = [last.at[0], last.at[1]]
    choices = [ref.at[pl.ds(span[0], span[1])] for ref in refs] + came
    index = route(mode, here, winner)
    for k in range(count):
        for i, ref in enumerate(choices):

            @pl.when(index[k] == i)
            def _():
                pltpu.make_async_copy(ref, stage.at[k], sems.at[k]).start()

    for k in range(count):
        pltpu.make_async_copy(choices[0], stage.at[k], sems.at[k]).wait()
        pltpu.make_async_copy(stage.at[k], outs[k], sems.at[4 + k]).start()
    for k in range(count):
        pltpu.make_async_copy(stage.at[k], outs[k], sems.at[4 + k]).wait()


def pick(mode, here, winner, arrays, span=None):
    rows, width = arrays[0].shape
    span = span or (0, rows)
    kind = arrays[0].dtype
    count = 2 if mode == "cross" else 4
    shape = (span[1], width)
    smem = pl.BlockSpec(memory_space=pltpu.SMEM)
    anywhere = pl.BlockSpec(memory_space=pl.ANY)
    if mode == "gather":
        out_shape, out_specs = [jax.ShapeDtypeStruct(shape, kind)] * 4, [anywhere] * 4
    else:
        out_shape, out_specs = jax.ShapeDtypeStruct((count,) + shape, kind), anywhere
    return pl.pallas_call(
        functools.partial(pick_kernel, mode, span),
        in_specs=[smem, smem] + [anywhere] * len(arrays),
        out_specs=out_specs,
        out_shape=out_shape,
        scratch_shapes=[
            pltpu.VMEM((count,) + shape, kind),
            pltpu.SemaphoreType.DMA((8,)),
        ],
        compiler_params=pltpu.CompilerParams(vmem_limit_bytes=16 * 2**20),
        cost_estimate=pl.CostEstimate(
            flops=0, bytes_accessed=4 * count * span[1] * width, transcendentals=0
        ),
    )(here, winner, *arrays)


def spread(pieces):
    return [lax.ppermute(pieces[j], "member", along_row(j)) for j in (1, 2, 3)]


def body(
    tokens,
    cotangent,
    gate_weight,
    up_weight,
    gate_first,
    up_first,
    gate_second,
    up_second,
    winner,
    rate_index,
):
    sync = lax.optimization_barrier
    own = tokens[0]
    count, width = own.shape
    hidden = gate_weight.shape[1]
    scale = width ** (-0.5)
    here = jnp.stack([lax.axis_index("member"), lax.axis_index("fsdp")]).astype(jnp.int32)
    learning = 0.2 * jnp.exp2(
        (rate_index[lax.axis_index("member")].astype(jnp.float32) - 2.0) * 0.5
    )
    rate = jnp.full((1,), learning, jnp.float32)

    def fsdp(value, pairs):
        return lax.ppermute(value, "fsdp", pairs)

    def exchange(held, span=None):
        return lax.ppermute(pick("cross", here, winner, held, span), "member", row_swap)

    def gathered(held, came):
        sent = pick("gather", here, winner, [*held, came])
        return [sent[0], *spread(sent)]

    def columns(held, came, span):
        return lax.all_to_all(
            pick("columns", here, winner, [*held, came], span),
            "member",
            0,
            0,
            axis_index_groups=rows_of_members,
            tiled=True,
        )

    half = hidden // 2
    spans = [(0, half), (half, half)]
    weights = [w[0, k * half : (k + 1) * half] for w in (gate_weight, up_weight) for k in range(2)]
    moments = [m[0] for m in (gate_first, up_first, gate_second, up_second)]
    with jax.named_scope("tick_a"):
        held0 = [weights[0], *spread(weights)]
        partner = fsdp(own, low_swap)
    partner, held0, own, turned, moments = sync((partner, held0, own, cotangent[0], moments))
    with jax.named_scope("tick_b"):
        came0 = exchange(held0)
        near = [lax.ppermute(moments[j], "member", along_row(j)) for j in (1, 3)]
        start = jnp.concatenate([own, partner])
        up1, down1 = fsdp(start, z_up), fsdp(start, z_down)
        turned = turned.T.reshape(16, 2 * hidden, count)
        cots = lax.all_to_all(turned, "fsdp", 0, 0, axis_index_groups=same_core, tiled=True)
    up1, down1, came0, held0, near, moments = sync((up1, down1, came0, held0, near, moments))
    with jax.named_scope("tick_b"):
        up2, down2 = fsdp(up1, z_up), fsdp(down1, z_down)
        far = lax.ppermute(moments[2], "member", along_row(2))
        held1 = [moments[0], near[0], far, near[1]]
    up2, down2, came0, held0, held1 = sync((up2, down2, came0, held0, held1))
    with jax.named_scope("tick_c"):
        up3, down3 = fsdp(up2, z_up), fsdp(down2, z_down)
        got0 = gathered(held0, came0)
        came1 = exchange(held1, spans[0])
    up3, down3, got0, came1, held1, cots = sync((up3, down3, got0, came1, held1, cots))
    with jax.named_scope("tick_d"):
        mine = pick("place", here, winner, got0).reshape(2, hidden, width)
        theirs = fsdp(mine, core_swap)
        got1 = columns(held1, came1, spans[0])
        came2 = exchange(held1, spans[1])
        sides = [fsdp(up3[:count], z_up), fsdp(down3[count:], z_down)]
        blocks = [start, up1, down1, up2, down2]
        sources = [(d, b) for d in (0, -1, 1, -2, 2) for b in range(2)]
        totals = terms(here, mine, theirs, cots, blocks, sources, None, scale)
    sides, came2, totals, got1, held1 = sync((sides, came2, totals, got1, held1))
    with jax.named_scope("tick_e"):
        got2 = columns(held1, came2, spans[1])
        sources = [(d, b) for d in (-3, 3, 4) for b in range(2)]
        sums = terms(here, mine, theirs, cots, [up3, down3, *sides], sources, totals, scale)
        other = [fsdp(part, core_swap) for part in sums[2:]]
    with jax.named_scope("adam"):
        new = adam(here, winner, rate, mine, got1, sums[:2], other[0::2], scale, 0, [])
        return tuple(adam(here, winner, rate, mine, got2, sums[:2], other[1::2], scale, 1, new))


def solution(mesh):
    split = P("member", "fsdp", None)
    return jax.shard_map(
        body,
        mesh=mesh,
        in_specs=(split,) * 8 + (P(), P()),
        out_specs=(split,) * 6,
        check_vma=False,
    )
```

```python
import functools

import jax
import jax.numpy as jnp
from jax import lax
from jax.experimental import pallas as pl
from jax.experimental.pallas import tpu as pltpu
from jax.sharding import PartitionSpec as P

gelu_c = 0.7978845608028654
bias_first = 1.0 - 0.9**10
bias_second = 1.0 - 0.95**10
nz = 8
tile = 256


def device(z, low, core):
    return (z * 2 + low) * 2 + core


everyone = [(z, low, core) for z in range(nz) for low in range(2) for core in range(2)]
z_up = [(device(z, a, c), device((z + 1) % nz, a, c)) for z, a, c in everyone]
z_down = [(b, a) for a, b in z_up]
core_swap = [(i, i ^ 1) for i in range(32)]
same_core = [[i for i in range(32) if i % 2 == core] for core in range(2)]
low_swap = [(i, i ^ 2) for i in range(32)]
row_swap = [(m, m ^ 1) for m in range(8)]


rows_of_members = [[m for m in range(8) if m % 2 == row] for row in range(2)]


def along_row(hops):
    return [(m, (m + 2 * hops) % 8) for m in range(8)]


def gelu_parts(gate_pre):
    tangent = jnp.tanh(gelu_c * (gate_pre + 0.044715 * gate_pre * gate_pre * gate_pre))
    activated = 0.5 * gate_pre * (1.0 + tangent)
    slope = 0.5 * (1.0 + tangent) + 0.5 * gate_pre * (1.0 - tangent * tangent) * gelu_c * (
        1.0 + 3.0 * 0.044715 * gate_pre * gate_pre
    )
    return (activated, slope)


def launch(copies):
    for copy in copies:
        copy.start()
    for copy in copies:
        copy.wait()


def terms_kernel(lengths, sources, first, scale, here, mine, theirs, cots, *refs):
    count = len(lengths)
    tokens, refs = refs[:count], refs[count:]
    if not first:
        kept, sent, refs = refs[:2], refs[2:6], refs[6:]
    keep, send = refs[:2], refs[2:6]
    x, c, w, grad, cot, sems = refs[6:]
    rows, hidden = mine.shape[1], 2 * mine.shape[1]
    half = rows // 2
    me = here[1]
    z, low, core = me // 4, (me // 2) % 2, me % 2
    mine_at = pl.multiple_of(core * rows, 32)
    theirs_at = pl.multiple_of((1 - core) * rows, 32)
    pairs = []
    for p in range(2):
        pairs.append((mine.at[p], w.at[pl.ds(p * hidden + mine_at, rows)]))
        pairs.append((theirs.at[p], w.at[pl.ds(p * hidden + theirs_at, rows)]))
    at = 0
    for ref, length in zip(tokens, lengths):
        pairs.append((ref, x.at[pl.ds(at, length)]))
        at += length
    for k, (hops, other) in enumerate(sources):
        source = ((z + hops + nz) % nz) * 2 + (low + other) % 2
        pairs.append((cots.at[source], c.at[k]))
    ready = len(pairs)
    if not first:
        for p in range(2):
            pairs.append((kept[p], grad.at[pl.ds(p * hidden + mine_at, rows)]))
            for h in range(2):
                to = p * hidden + theirs_at + h * half
                pairs.append((sent[2 * p + h], grad.at[pl.ds(to, half)]))
    copies = [pltpu.make_async_copy(a, b, sems.at[k]) for k, (a, b) in enumerate(pairs)]
    for copy in copies:
        copy.start()
    for copy in copies[:ready]:
        copy.wait()

    @pl.loop(0, x.shape[0] // tile)
    def _(t):
        block = x[pl.ds(pl.multiple_of(t * tile, tile), tile), :]
        pre = (
            lax.dot_general(
                w[...], block, (((1,), (1,)), ((), ())), preferred_element_type=jnp.float32
            )
            * scale
        )
        value = jnp.concatenate([c[2 * t], c[2 * t + 1]], axis=1).astype(jnp.float32)
        activated, slope = gelu_parts(pre[:hidden])
        columns = pl.ds(pl.multiple_of(t * tile, tile), tile)
        cot[pl.ds(0, hidden), columns] = (value * pre[hidden:] * slope).astype(jnp.bfloat16)
        cot[pl.ds(hidden, hidden), columns] = (value * activated).astype(jnp.bfloat16)

    for copy in copies[ready:]:
        copy.wait()

    @pl.loop(0, x.shape[1] // tile)
    def _(n):
        columns = pl.ds(pl.multiple_of(n * tile, tile), tile)
        part = jnp.dot(cot[...], x[:, columns], preferred_element_type=jnp.float32)
        if first:
            grad[:, columns] = part
        else:
            grad[:, columns] += part

    outs = []
    for p in range(2):
        for h in range(2):
            to = p * hidden + theirs_at + h * half
            outs.append((grad.at[pl.ds(to, half)], send[2 * p + h]))
        outs.append((grad.at[pl.ds(p * hidden + mine_at, rows)], keep[p]))
    launch([pltpu.make_async_copy(a, b, sems.at[k]) for k, (a, b) in enumerate(outs)])


def terms(here, mine, theirs, cots, blocks, sources, totals, scale):
    rows, width = mine.shape[1], mine.shape[2]
    total = sum(b.shape[0] for b in blocks)
    first = totals is None
    anywhere = pl.BlockSpec(memory_space=pl.ANY)
    args = [mine, theirs, cots, *blocks, *([] if first else totals)]
    sums = jax.ShapeDtypeStruct((rows, width), jnp.float32)
    parts = jax.ShapeDtypeStruct((rows // 2, width), jnp.float32)
    kernel = functools.partial(
        terms_kernel, tuple(b.shape[0] for b in blocks), tuple(sources), first, scale
    )
    return pl.pallas_call(
        kernel,
        in_specs=[pl.BlockSpec(memory_space=pltpu.SMEM)] + [anywhere] * len(args),
        out_specs=[anywhere] * 6,
        out_shape=[sums] * 2 + [parts] * 4,
        scratch_shapes=[
            pltpu.VMEM((total, width), jnp.bfloat16),
            pltpu.VMEM((len(sources), 2 * rows, cots.shape[2]), jnp.bfloat16),
            pltpu.VMEM((4 * rows, width), jnp.bfloat16),
            pltpu.VMEM((4 * rows, width), jnp.float32),
            pltpu.VMEM((4 * rows, total), jnp.bfloat16),
            pltpu.SemaphoreType.DMA((10 + len(blocks) + len(sources),)),
        ],
        compiler_params=pltpu.CompilerParams(vmem_limit_bytes=60 * 2**20),
        cost_estimate=pl.CostEstimate(
            flops=16 * rows * width * total,
            bytes_accessed=20 * 2**20,
            transcendentals=2 * rows * total,
        ),
    )(here, *args)


def moved(here, winner, part):
    source = winner[here[0]]
    return (here[0] // 2 - source // 2 - part + 8) % 4


def adam_kernel(scale, here, winner, rate, w_ref, *refs):
    got, kept, came, outs = refs[:2], refs[2:4], refs[4:8], refs[8:]
    learning = rate[0]
    column = winner[here[0]] // 2
    early = pl.program_id(0) < pl.num_programs(0) // 2

    def moment(part):
        which = (column + part) % 4
        return jnp.where(early, got[0][which], got[1][which]).astype(jnp.float32)

    for p in range(2):
        sent = jnp.where(early, came[2 * p][...], came[2 * p + 1][...])
        grad = (kept[p][...] + sent) * scale
        first_new = 0.9 * moment(p) + 0.1 * grad
        second_new = 0.95 * moment(2 + p) + 0.05 * grad * grad
        update = learning * (first_new / bias_first) / (jnp.sqrt(second_new / bias_second) + 1e-08)
        outs[p][0] = (w_ref[p].astype(jnp.float32) - update).astype(jnp.bfloat16)
        outs[2 + p][0] = first_new.astype(jnp.bfloat16)
        outs[4 + p][0] = second_new.astype(jnp.bfloat16)


def adam(here, winner, rate, weights, got, mine, other, scale):
    hidden, width = weights.shape[1], weights.shape[2]
    rows = 16
    steps = hidden // rows
    middle = steps // 2

    def first_half(i):
        return jnp.minimum(i, middle - 1)

    def second_half(i):
        return jnp.maximum(i - middle, 0)

    pair = pl.BlockSpec((2, rows, width), lambda i, *_: (0, i, 0))
    flat = pl.BlockSpec((rows, width), lambda i, *_: (i, 0))
    one = pl.BlockSpec((1, rows, width), lambda i, *_: (0, i, 0))
    fours = [
        pl.BlockSpec((4, rows, width), lambda i, *_: (0, first_half(i), 0)),
        pl.BlockSpec((4, rows, width), lambda i, *_: (0, second_half(i), 0)),
    ]
    pieces = [
        pl.BlockSpec((rows, width), lambda i, *_: (first_half(i), 0)),
        pl.BlockSpec((rows, width), lambda i, *_: (second_half(i), 0)),
    ]
    return pl.pallas_call(
        functools.partial(adam_kernel, scale),
        grid_spec=pltpu.PrefetchScalarGridSpec(
            num_scalar_prefetch=3,
            grid=(steps,),
            in_specs=[pair, *fours, flat, flat, *pieces, *pieces],
            out_specs=[one] * 6,
        ),
        out_shape=[jax.ShapeDtypeStruct((1, hidden, width), jnp.bfloat16)] * 6,
        compiler_params=pltpu.CompilerParams(vmem_limit_bytes=60 * 2**20),
    )(here, winner, rate, weights, *got, *mine, *other)


def losers(winner):
    low, high = 0, 0
    for m in range(7, -1, -1):
        low = jnp.where(winner[m] != m, m, low)
    for m in range(8):
        high = jnp.where(winner[m] != m, m, high)
    return low, high


def route(mode, here, winner):
    member = here[0]
    column, row = member // 2, member % 2
    low, high = losers(winner)
    if mode == "cross":
        return [(column - winner[m] // 2 + 4) % 4 for m in (low, high)]
    if mode == "place":
        return [moved(here, winner, part) for part in range(4)]
    wanted = []
    for j in range(4):
        target = j * 2 + row if mode == "columns" else ((column + j) % 4) * 2 + row
        source = winner[target]
        inside = (column - source // 2 + 4) % 4
        outside = jnp.where(target == low, 4, 5)
        wanted.append(jnp.where(source % 2 == row, inside, outside))
    return wanted


def pick_kernel(mode, here, winner, *refs):
    count = 2 if mode == "cross" else 4
    stage, sems = refs[-2:]
    if mode == "gather":
        outs, refs = list(refs[-6:-2]), list(refs[:-6])
    else:
        outs, refs = [refs[-3].at[k] for k in range(count)], list(refs[:-3])
    came = []
    if mode in ("gather", "columns"):
        last = refs.pop()
        came = [last.at[0], last.at[1]]
    choices = refs + came
    index = route(mode, here, winner)
    for k in range(count):
        for i, ref in enumerate(choices):

            @pl.when(index[k] == i)
            def _():
                pltpu.make_async_copy(ref, stage.at[k], sems.at[k]).start()

    for k in range(count):
        pltpu.make_async_copy(choices[0], stage.at[k], sems.at[k]).wait()
        pltpu.make_async_copy(stage.at[k], outs[k], sems.at[4 + k]).start()
    for k in range(count):
        pltpu.make_async_copy(stage.at[k], outs[k], sems.at[4 + k]).wait()


def pick(mode, here, winner, arrays):
    shape = arrays[0].shape
    kind = arrays[0].dtype
    count = 2 if mode == "cross" else 4
    smem = pl.BlockSpec(memory_space=pltpu.SMEM)
    anywhere = pl.BlockSpec(memory_space=pl.ANY)
    if mode == "gather":
        out_shape, out_specs = [jax.ShapeDtypeStruct(shape, kind)] * 4, [anywhere] * 4
    else:
        out_shape, out_specs = jax.ShapeDtypeStruct((count,) + shape, kind), anywhere
    return pl.pallas_call(
        functools.partial(pick_kernel, mode),
        in_specs=[smem, smem] + [anywhere] * len(arrays),
        out_specs=out_specs,
        out_shape=out_shape,
        scratch_shapes=[
            pltpu.VMEM((count,) + shape, kind),
            pltpu.SemaphoreType.DMA((8,)),
        ],
        compiler_params=pltpu.CompilerParams(vmem_limit_bytes=60 * 2**20),
        cost_estimate=pl.CostEstimate(
            flops=0, bytes_accessed=4 * count * arrays[0].size, transcendentals=0
        ),
    )(here, winner, *arrays)


def spread(pieces):
    return [lax.ppermute(pieces[j], "member", along_row(j)) for j in (1, 2, 3)]


def body(
    tokens,
    cotangent,
    gate_weight,
    up_weight,
    gate_first,
    up_first,
    gate_second,
    up_second,
    winner,
    rate_index,
):
    sync = lax.optimization_barrier
    own = tokens[0]
    count, width = own.shape
    hidden = gate_weight.shape[1]
    scale = width ** (-0.5)
    here = jnp.stack([lax.axis_index("member"), lax.axis_index("fsdp")]).astype(jnp.int32)
    learning = 0.2 * jnp.exp2(
        (rate_index[lax.axis_index("member")].astype(jnp.float32) - 2.0) * 0.5
    )
    rate = jnp.full((1,), learning, jnp.float32)

    def fsdp(value, pairs):
        return lax.ppermute(value, "fsdp", pairs)

    def exchange(held):
        return lax.ppermute(pick("cross", here, winner, held), "member", row_swap)

    def gathered(held, came):
        sent = pick("gather", here, winner, [*held, came])
        return [sent[0], *spread(sent)]

    def columns(held, came):
        return lax.all_to_all(
            pick("columns", here, winner, [*held, came]),
            "member",
            0,
            0,
            axis_index_groups=rows_of_members,
            tiled=True,
        )

    def rows_of(array, k):
        half = hidden // 2
        return array[0, k * half : (k + 1) * half]

    weights = [rows_of(w, k) for w in (gate_weight, up_weight) for k in range(2)]
    moments = [
        [rows_of(m, k) for m in (gate_first, up_first, gate_second, up_second)] for k in range(2)
    ]
    with jax.named_scope("tick_a"):
        partner = fsdp(own, low_swap)
        turned = cotangent[0].T
    partner, turned, own, weights = sync((partner, turned, own, weights))
    with jax.named_scope("tick_a"):
        start = jnp.concatenate([own, partner])
        up1, down1 = fsdp(start, z_up), fsdp(start, z_down)
        held0 = [weights[0], *spread(weights)]
    up1, down1, held0, turned, moments[0] = sync((up1, down1, held0, turned, moments[0]))
    with jax.named_scope("tick_b"):
        up2, down2 = fsdp(up1, z_up), fsdp(down1, z_down)
        came0 = exchange(held0)
        turned = turned.reshape(16, 2 * hidden, count)
        cots = lax.all_to_all(turned, "fsdp", 0, 0, axis_index_groups=same_core, tiled=True)
        held1 = [moments[0][0], *spread(moments[0])]
    came0, held0, held1, moments[1] = sync((came0, held0, held1, moments[1]))
    with jax.named_scope("tick_c"):
        got0 = gathered(held0, came0)
    got0, held1, moments[1] = sync((got0, held1, moments[1]))
    with jax.named_scope("tick_c"):
        came1 = exchange(held1)
        held2 = [moments[1][0], *spread(moments[1])]
    up2, down2, got0, came1, held1, held2, cots = sync(
        (up2, down2, got0, came1, held1, held2, cots)
    )
    with jax.named_scope("tick_d"):
        up3, down3 = fsdp(up2, z_up), fsdp(down2, z_down)
        mine = pick("place", here, winner, got0).reshape(2, hidden, width)
        theirs = fsdp(mine, core_swap)
        got1 = columns(held1, came1)
        came2 = exchange(held2)
        blocks = [start, up1, down1, up2, down2]
        sources = [(d, b) for d in (0, -1, 1, -2, 2) for b in range(2)]
        totals = terms(here, mine, theirs, cots, blocks, sources, None, scale)
    up3, down3, came2, totals, got1, held2 = sync((up3, down3, came2, totals, got1, held2))
    with jax.named_scope("tick_e"):
        sides = [fsdp(up3[:count], z_up), fsdp(down3[count:], z_down)]
        got2 = columns(held2, came2)
        sources = [(d, b) for d in (-3, 3, 4) for b in range(2)]
        sums = terms(here, mine, theirs, cots, [up3, down3, *sides], sources, totals, scale)
        other = [fsdp(part, core_swap) for part in sums[2:]]
    with jax.named_scope("adam"):
        return tuple(adam(here, winner, rate, mine, [got1, got2], sums[:2], other, scale))


def solution(mesh):
    split = P("member", "fsdp", None)
    return jax.shard_map(
        body,
        mesh=mesh,
        in_specs=(split,) * 8 + (P(), P()),
        out_specs=(split,) * 6,
        check_vma=False,
    )
```

```python
import functools

import jax
import jax.numpy as jnp
from jax import lax
from jax.experimental import pallas as pl
from jax.experimental.pallas import tpu as pltpu
from jax.sharding import PartitionSpec as P

gelu_c = 0.7978845608028654
bias_first = 1.0 - 0.9**10
bias_second = 1.0 - 0.95**10
nz = 8
tile = 256


def device(z, low, core):
    return (z * 2 + low) * 2 + core


everyone = [(z, low, core) for z in range(nz) for low in range(2) for core in range(2)]
z_up = [(device(z, a, c), device((z + 1) % nz, a, c)) for z, a, c in everyone]
z_down = [(b, a) for a, b in z_up]
core_swap = [(i, i ^ 1) for i in range(32)]
same_core = [[i for i in range(32) if i % 2 == core] for core in range(2)]
low_swap = [(i, i ^ 2) for i in range(32)]
row_swap = [(m, m ^ 1) for m in range(8)]


rows_of_members = [[m for m in range(8) if m % 2 == row] for row in range(2)]


def along_row(hops):
    return [(m, (m + 2 * hops) % 8) for m in range(8)]


def gelu_parts(gate_pre):
    tangent = jnp.tanh(gelu_c * (gate_pre + 0.044715 * gate_pre * gate_pre * gate_pre))
    activated = 0.5 * gate_pre * (1.0 + tangent)
    slope = 0.5 * (1.0 + tangent) + 0.5 * gate_pre * (1.0 - tangent * tangent) * gelu_c * (
        1.0 + 3.0 * 0.044715 * gate_pre * gate_pre
    )
    return (activated, slope)


def launch(copies):
    for copy in copies:
        copy.start()
    for copy in copies:
        copy.wait()


def terms_kernel(lengths, sources, first, scale, here, mine, theirs, cots, *refs):
    count = len(lengths)
    tokens, refs = refs[:count], refs[count:]
    if not first:
        kept, sent, refs = refs[:2], refs[2:6], refs[6:]
    keep, send = refs[:2], refs[2:6]
    x, c, w, grad, cot, sems = refs[6:]
    rows, hidden = mine.shape[1], 2 * mine.shape[1]
    half = mine.shape[2] // 2
    me = here[1]
    z, low, core = me // 4, (me // 2) % 2, me % 2
    mine_at = pl.multiple_of(core * rows, 32)
    theirs_at = pl.multiple_of((1 - core) * rows, 32)
    pairs = []
    for p in range(2):
        pairs.append((mine.at[p], w.at[pl.ds(p * hidden + mine_at, rows)]))
        pairs.append((theirs.at[p], w.at[pl.ds(p * hidden + theirs_at, rows)]))
    at = 0
    for ref, length in zip(tokens, lengths):
        pairs.append((ref, x.at[pl.ds(at, length)]))
        at += length
    for k, (hops, other) in enumerate(sources):
        source = ((z + hops + nz) % nz) * 2 + (low + other) % 2
        pairs.append((cots.at[source], c.at[k]))
    ready = len(pairs)
    if not first:
        for p in range(2):
            pairs.append((kept[p], grad.at[pl.ds(p * hidden + mine_at, rows)]))
            for h in range(2):
                to = (pl.ds(p * hidden + theirs_at, rows), pl.ds(h * half, half))
                pairs.append((sent[2 * p + h], grad.at[to]))
    copies = [pltpu.make_async_copy(a, b, sems.at[k]) for k, (a, b) in enumerate(pairs)]
    for copy in copies:
        copy.start()
    for copy in copies[:ready]:
        copy.wait()

    @pl.loop(0, x.shape[0] // tile)
    def _(t):
        block = x[pl.ds(pl.multiple_of(t * tile, tile), tile), :]
        pre = (
            lax.dot_general(
                w[...], block, (((1,), (1,)), ((), ())), preferred_element_type=jnp.float32
            )
            * scale
        )
        value = jnp.concatenate([c[2 * t], c[2 * t + 1]], axis=1).astype(jnp.float32)
        activated, slope = gelu_parts(pre[:hidden])
        columns = pl.ds(pl.multiple_of(t * tile, tile), tile)
        cot[pl.ds(0, hidden), columns] = (value * pre[hidden:] * slope).astype(jnp.bfloat16)
        cot[pl.ds(hidden, hidden), columns] = (value * activated).astype(jnp.bfloat16)

    for copy in copies[ready:]:
        copy.wait()

    @pl.loop(0, x.shape[1] // tile)
    def _(n):
        columns = pl.ds(pl.multiple_of(n * tile, tile), tile)
        part = jnp.dot(cot[...], x[:, columns], preferred_element_type=jnp.float32)
        if first:
            grad[:, columns] = part
        else:
            grad[:, columns] += part

    outs = []
    for p in range(2):
        for h in range(2):
            to = (pl.ds(p * hidden + theirs_at, rows), pl.ds(h * half, half))
            outs.append((grad.at[to], send[2 * p + h]))
        outs.append((grad.at[pl.ds(p * hidden + mine_at, rows)], keep[p]))
    launch([pltpu.make_async_copy(a, b, sems.at[k]) for k, (a, b) in enumerate(outs)])


def terms(here, mine, theirs, cots, blocks, sources, totals, scale):
    rows, width = mine.shape[1], mine.shape[2]
    total = sum(b.shape[0] for b in blocks)
    first = totals is None
    anywhere = pl.BlockSpec(memory_space=pl.ANY)
    args = [mine, theirs, cots, *blocks, *([] if first else totals)]
    sums = jax.ShapeDtypeStruct((rows, width), jnp.float32)
    parts = jax.ShapeDtypeStruct((rows, width // 2), jnp.float32)
    kernel = functools.partial(
        terms_kernel, tuple(b.shape[0] for b in blocks), tuple(sources), first, scale
    )
    return pl.pallas_call(
        kernel,
        in_specs=[pl.BlockSpec(memory_space=pltpu.SMEM)] + [anywhere] * len(args),
        out_specs=[anywhere] * 6,
        out_shape=[sums] * 2 + [parts] * 4,
        scratch_shapes=[
            pltpu.VMEM((total, width), jnp.bfloat16),
            pltpu.VMEM((len(sources), 2 * rows, cots.shape[2]), jnp.bfloat16),
            pltpu.VMEM((4 * rows, width), jnp.bfloat16),
            pltpu.VMEM((4 * rows, width), jnp.float32),
            pltpu.VMEM((4 * rows, total), jnp.bfloat16),
            pltpu.SemaphoreType.DMA((10 + len(blocks) + len(sources),)),
        ],
        compiler_params=pltpu.CompilerParams(vmem_limit_bytes=60 * 2**20),
        cost_estimate=pl.CostEstimate(
            flops=16 * rows * width * total,
            bytes_accessed=20 * 2**20,
            transcendentals=2 * rows * total,
        ),
    )(here, *args)


def moved(here, winner, part):
    source = winner[here[0]]
    return (here[0] // 2 - source // 2 - part + 8) % 4


def adam_kernel(scale, here, winner, rate, w_ref, *refs):
    got, kept, came, outs = refs[:2], refs[2:4], refs[4:8], refs[8:]
    learning = rate[0]
    column = winner[here[0]] // 2

    def moment(part):
        which = (column + part) % 4
        return jnp.concatenate([got[0][which], got[1][which]], axis=1).astype(jnp.float32)

    for p in range(2):
        sent = jnp.concatenate([came[2 * p][...], came[2 * p + 1][...]], axis=1)
        grad = (kept[p][...] + sent) * scale
        first_new = 0.9 * moment(p) + 0.1 * grad
        second_new = 0.95 * moment(2 + p) + 0.05 * grad * grad
        update = learning * (first_new / bias_first) / (jnp.sqrt(second_new / bias_second) + 1e-08)
        outs[p][0] = (w_ref[p].astype(jnp.float32) - update).astype(jnp.bfloat16)
        outs[2 + p][0] = first_new.astype(jnp.bfloat16)
        outs[4 + p][0] = second_new.astype(jnp.bfloat16)


def adam(here, winner, rate, weights, got, mine, other, scale):
    hidden, width = weights.shape[1], weights.shape[2]
    rows = 32
    pair = pl.BlockSpec((2, rows, width), lambda i, *_: (0, i, 0))
    four = pl.BlockSpec((4, rows, width // 2), lambda i, *_: (0, i, 0))
    flat = pl.BlockSpec((rows, width), lambda i, *_: (i, 0))
    piece = pl.BlockSpec((rows, width // 2), lambda i, *_: (i, 0))
    one = pl.BlockSpec((1, rows, width), lambda i, *_: (0, i, 0))
    return pl.pallas_call(
        functools.partial(adam_kernel, scale),
        grid_spec=pltpu.PrefetchScalarGridSpec(
            num_scalar_prefetch=3,
            grid=(hidden // rows,),
            in_specs=[pair] + [four] * 2 + [flat] * 2 + [piece] * 4,
            out_specs=[one] * 6,
        ),
        out_shape=[jax.ShapeDtypeStruct((1, hidden, width), jnp.bfloat16)] * 6,
        compiler_params=pltpu.CompilerParams(vmem_limit_bytes=60 * 2**20),
    )(here, winner, rate, weights, *got, *mine, *other)


def losers(winner):
    low, high = 0, 0
    for m in range(7, -1, -1):
        low = jnp.where(winner[m] != m, m, low)
    for m in range(8):
        high = jnp.where(winner[m] != m, m, high)
    return low, high


def route(mode, here, winner):
    member = here[0]
    column, row = member // 2, member % 2
    low, high = losers(winner)
    if mode == "cross":
        return [(column - winner[m] // 2 + 4) % 4 for m in (low, high)]
    if mode == "place":
        return [moved(here, winner, part) for part in range(4)]
    wanted = []
    for j in range(4):
        target = j * 2 + row if mode == "columns" else ((column + j) % 4) * 2 + row
        source = winner[target]
        inside = (column - source // 2 + 4) % 4
        outside = jnp.where(target == low, 4, 5)
        wanted.append(jnp.where(source % 2 == row, inside, outside))
    return wanted


def pick_kernel(mode, span, here, winner, *refs):
    count = 2 if mode == "cross" else 4
    stage, sems = refs[-2:]
    if mode == "gather":
        outs, refs = list(refs[-6:-2]), list(refs[:-6])
    else:
        outs, refs = [refs[-3].at[k] for k in range(count)], list(refs[:-3])
    came = []
    if mode in ("gather", "columns"):
        last = refs.pop()
        came = [last.at[0], last.at[1]]
    choices = [ref.at[:, pl.ds(span[0], span[1])] if span else ref for ref in refs] + came
    index = route(mode, here, winner)
    for k in range(count):
        for i, ref in enumerate(choices):

            @pl.when(index[k] == i)
            def _():
                pltpu.make_async_copy(ref, stage.at[k], sems.at[k]).start()

    for k in range(count):
        pltpu.make_async_copy(choices[0], stage.at[k], sems.at[k]).wait()
        pltpu.make_async_copy(stage.at[k], outs[k], sems.at[4 + k]).start()
    for k in range(count):
        pltpu.make_async_copy(stage.at[k], outs[k], sems.at[4 + k]).wait()


def pick(mode, here, winner, arrays, span=None):
    rows, width = arrays[0].shape
    shape = (rows, span[1] if span else width)
    kind = arrays[0].dtype
    count = 2 if mode == "cross" else 4
    smem = pl.BlockSpec(memory_space=pltpu.SMEM)
    anywhere = pl.BlockSpec(memory_space=pl.ANY)
    if mode == "gather":
        out_shape, out_specs = [jax.ShapeDtypeStruct(shape, kind)] * 4, [anywhere] * 4
    else:
        out_shape, out_specs = jax.ShapeDtypeStruct((count,) + shape, kind), anywhere
    return pl.pallas_call(
        functools.partial(pick_kernel, mode, span),
        in_specs=[smem, smem] + [anywhere] * len(arrays),
        out_specs=out_specs,
        out_shape=out_shape,
        scratch_shapes=[
            pltpu.VMEM((count,) + shape, kind),
            pltpu.SemaphoreType.DMA((8,)),
        ],
        compiler_params=pltpu.CompilerParams(vmem_limit_bytes=60 * 2**20),
        cost_estimate=pl.CostEstimate(
            flops=0, bytes_accessed=4 * count * arrays[0].size, transcendentals=0
        ),
    )(here, winner, *arrays)


def spread(pieces):
    return [lax.ppermute(pieces[j], "member", along_row(j)) for j in (1, 2, 3)]


def body(
    tokens,
    cotangent,
    gate_weight,
    up_weight,
    gate_first,
    up_first,
    gate_second,
    up_second,
    winner,
    rate_index,
):
    sync = lax.optimization_barrier
    own = tokens[0]
    count, width = own.shape
    hidden = gate_weight.shape[1]
    scale = width ** (-0.5)
    here = jnp.stack([lax.axis_index("member"), lax.axis_index("fsdp")]).astype(jnp.int32)
    learning = 0.2 * jnp.exp2(
        (rate_index[lax.axis_index("member")].astype(jnp.float32) - 2.0) * 0.5
    )
    rate = jnp.full((1,), learning, jnp.float32)

    def fsdp(value, pairs):
        return lax.ppermute(value, "fsdp", pairs)

    def exchange(held, span=None):
        return lax.ppermute(pick("cross", here, winner, held, span), "member", row_swap)

    def gathered(held, came):
        sent = pick("gather", here, winner, [*held, came])
        return [sent[0], *spread(sent)]

    def columns(held, came, span):
        return lax.all_to_all(
            pick("columns", here, winner, [*held, came], span),
            "member",
            0,
            0,
            axis_index_groups=rows_of_members,
            tiled=True,
        )

    half = hidden // 2
    spans = [(0, width // 2), (width // 2, width // 2)]
    weights = [w[0, k * half : (k + 1) * half] for w in (gate_weight, up_weight) for k in range(2)]
    moments = [m[0] for m in (gate_first, up_first, gate_second, up_second)]
    turned = cotangent[0].T.reshape(16, 2 * hidden, count)
    with jax.named_scope("tick_a"):
        cots = lax.all_to_all(turned, "fsdp", 0, 0, axis_index_groups=same_core, tiled=True)
        start = jnp.concatenate([own, fsdp(own, low_swap)])
        held0 = [weights[0], *spread(weights)]
    start, held0, moments = sync((start, held0, moments))
    with jax.named_scope("tick_b"):
        up1, down1 = fsdp(start, z_up), fsdp(start, z_down)
        came0 = exchange(held0)
        held1 = [moments[0], *spread(moments)]
    up1, down1, came0, held0, cots = sync((up1, down1, came0, held0, cots))
    with jax.named_scope("tick_c"):
        up2, down2 = fsdp(up1, z_up), fsdp(down1, z_down)
        got0 = gathered(held0, came0)
    up2, down2, got0, held1 = sync((up2, down2, got0, held1))
    with jax.named_scope("tick_d"):
        up3, down3 = fsdp(up2, z_up), fsdp(down2, z_down)
        came1 = exchange(held1, spans[0])
        mine = pick("place", here, winner, got0).reshape(2, hidden, width)
        theirs = fsdp(mine, core_swap)
        sources = [(d, b) for d in (0, -1, 1) for b in range(2)]
        sums = terms(here, mine, theirs, cots, [start, up1, down1], sources, None, scale)
    up3, down3, came1, sums, held1 = sync((up3, down3, came1, sums, held1))
    with jax.named_scope("tick_e"):
        sides = [fsdp(up3[:count], z_up), fsdp(down3[count:], z_down)]
        got1 = columns(held1, came1, spans[0])
        came2 = exchange(held1, spans[1])
        sources = [(d, b) for d in (-2, 2, -3, 3) for b in range(2)]
        sums = terms(here, mine, theirs, cots, [up2, down2, up3, down3], sources, sums, scale)
    sides, came2, sums, got1, held1 = sync((sides, came2, sums, got1, held1))
    with jax.named_scope("tick_f"):
        got2 = columns(held1, came2, spans[1])
        sources = [(4, b) for b in range(2)]
        sums = terms(here, mine, theirs, cots, sides, sources, sums, scale)
        other = [fsdp(part, core_swap) for part in sums[2:]]
    with jax.named_scope("adam"):
        return tuple(adam(here, winner, rate, mine, [got1, got2], sums[:2], other, scale))


def solution(mesh):
    split = P("member", "fsdp", None)
    return jax.shard_map(
        body,
        mesh=mesh,
        in_specs=(split,) * 8 + (P(), P()),
        out_specs=(split,) * 6,
        check_vma=False,
    )
```

```python
import functools

import jax
import jax.numpy as jnp
from jax import lax
from jax.experimental import pallas as pl
from jax.experimental.pallas import tpu as pltpu
from jax.sharding import PartitionSpec as P

gelu_c = 0.7978845608028654
bias_first = 1.0 - 0.9**10
bias_second = 1.0 - 0.95**10
nz = 8
tile = 256


def device(z, low, core):
    return (z * 2 + low) * 2 + core


everyone = [(z, low, core) for z in range(nz) for low in range(2) for core in range(2)]
z_up = [(device(z, a, c), device((z + 1) % nz, a, c)) for z, a, c in everyone]
z_down = [(b, a) for a, b in z_up]
core_swap = [(i, i ^ 1) for i in range(32)]
same_core = [[i for i in range(32) if i % 2 == core] for core in range(2)]
low_swap = [(i, i ^ 2) for i in range(32)]
row_swap = [(m, m ^ 1) for m in range(8)]


rows_of_members = [[m for m in range(8) if m % 2 == row] for row in range(2)]


def along_row(hops):
    return [(m, (m + 2 * hops) % 8) for m in range(8)]


def gelu_parts(gate_pre):
    tangent = jnp.tanh(gelu_c * (gate_pre + 0.044715 * gate_pre * gate_pre * gate_pre))
    activated = 0.5 * gate_pre * (1.0 + tangent)
    slope = 0.5 * (1.0 + tangent) + 0.5 * gate_pre * (1.0 - tangent * tangent) * gelu_c * (
        1.0 + 3.0 * 0.044715 * gate_pre * gate_pre
    )
    return (activated, slope)


def launch(copies):
    for copy in copies:
        copy.start()
    for copy in copies:
        copy.wait()


def terms_kernel(lengths, sources, first, scale, here, mine, theirs, cots, *refs):
    count = len(lengths)
    tokens, refs = refs[:count], refs[count:]
    if not first:
        kept, sent, refs = refs[:2], refs[2:6], refs[6:]
    keep, send = refs[:2], refs[2:6]
    x, c, w, grad, cot, sems = refs[6:]
    rows, hidden = mine.shape[1], 2 * mine.shape[1]
    half = mine.shape[2] // 2
    me = here[1]
    z, low, core = me // 4, (me // 2) % 2, me % 2
    mine_at = pl.multiple_of(core * rows, 32)
    theirs_at = pl.multiple_of((1 - core) * rows, 32)
    pairs = []
    for p in range(2):
        pairs.append((mine.at[p], w.at[pl.ds(p * hidden + mine_at, rows)]))
        pairs.append((theirs.at[p], w.at[pl.ds(p * hidden + theirs_at, rows)]))
    at = 0
    for ref, length in zip(tokens, lengths):
        pairs.append((ref, x.at[pl.ds(at, length)]))
        at += length
    for k, (hops, other) in enumerate(sources):
        source = ((z + hops + nz) % nz) * 2 + (low + other) % 2
        pairs.append((cots.at[source], c.at[k]))
    ready = len(pairs)
    if not first:
        for p in range(2):
            pairs.append((kept[p], grad.at[pl.ds(p * hidden + mine_at, rows)]))
            for h in range(2):
                to = (pl.ds(p * hidden + theirs_at, rows), pl.ds(h * half, half))
                pairs.append((sent[2 * p + h], grad.at[to]))
    copies = [pltpu.make_async_copy(a, b, sems.at[k]) for k, (a, b) in enumerate(pairs)]
    for copy in copies:
        copy.start()
    for copy in copies[:ready]:
        copy.wait()

    @pl.loop(0, x.shape[0] // tile)
    def _(t):
        block = x[pl.ds(pl.multiple_of(t * tile, tile), tile), :]
        pre = (
            lax.dot_general(
                w[...], block, (((1,), (1,)), ((), ())), preferred_element_type=jnp.float32
            )
            * scale
        )
        value = jnp.concatenate([c[2 * t], c[2 * t + 1]], axis=1).astype(jnp.float32)
        activated, slope = gelu_parts(pre[:hidden])
        columns = pl.ds(pl.multiple_of(t * tile, tile), tile)
        cot[pl.ds(0, hidden), columns] = (value * pre[hidden:] * slope).astype(jnp.bfloat16)
        cot[pl.ds(hidden, hidden), columns] = (value * activated).astype(jnp.bfloat16)

    for copy in copies[ready:]:
        copy.wait()

    @pl.loop(0, x.shape[1] // tile)
    def _(n):
        columns = pl.ds(pl.multiple_of(n * tile, tile), tile)
        part = jnp.dot(cot[...], x[:, columns], preferred_element_type=jnp.float32)
        if first:
            grad[:, columns] = part
        else:
            grad[:, columns] += part

    outs = []
    for p in range(2):
        for h in range(2):
            to = (pl.ds(p * hidden + theirs_at, rows), pl.ds(h * half, half))
            outs.append((grad.at[to], send[2 * p + h]))
        outs.append((grad.at[pl.ds(p * hidden + mine_at, rows)], keep[p]))
    launch([pltpu.make_async_copy(a, b, sems.at[k]) for k, (a, b) in enumerate(outs)])


def terms(here, mine, theirs, cots, blocks, sources, totals, scale):
    rows, width = mine.shape[1], mine.shape[2]
    total = sum(b.shape[0] for b in blocks)
    first = totals is None
    anywhere = pl.BlockSpec(memory_space=pl.ANY)
    args = [mine, theirs, cots, *blocks, *([] if first else totals)]
    sums = jax.ShapeDtypeStruct((rows, width), jnp.float32)
    parts = jax.ShapeDtypeStruct((rows, width // 2), jnp.float32)
    kernel = functools.partial(
        terms_kernel, tuple(b.shape[0] for b in blocks), tuple(sources), first, scale
    )
    return pl.pallas_call(
        kernel,
        in_specs=[pl.BlockSpec(memory_space=pltpu.SMEM)] + [anywhere] * len(args),
        out_specs=[anywhere] * 6,
        out_shape=[sums] * 2 + [parts] * 4,
        scratch_shapes=[
            pltpu.VMEM((total, width), jnp.bfloat16),
            pltpu.VMEM((len(sources), 2 * rows, cots.shape[2]), jnp.bfloat16),
            pltpu.VMEM((4 * rows, width), jnp.bfloat16),
            pltpu.VMEM((4 * rows, width), jnp.float32),
            pltpu.VMEM((4 * rows, total), jnp.bfloat16),
            pltpu.SemaphoreType.DMA((10 + len(blocks) + len(sources),)),
        ],
        compiler_params=pltpu.CompilerParams(vmem_limit_bytes=60 * 2**20),
        cost_estimate=pl.CostEstimate(
            flops=16 * rows * width * total,
            bytes_accessed=20 * 2**20,
            transcendentals=2 * rows * total,
        ),
    )(here, *args)


def moved(here, winner, part):
    source = winner[here[0]]
    return (here[0] // 2 - source // 2 - part + 8) % 4


def adam_kernel(scale, here, winner, rate, w_ref, *refs):
    got, kept, came, outs = refs[:2], refs[2:4], refs[4:8], refs[8:]
    learning = rate[0]
    column = winner[here[0]] // 2

    def moment(part):
        which = (column + part) % 4
        return jnp.concatenate([got[0][which], got[1][which]], axis=1).astype(jnp.float32)

    for p in range(2):
        sent = jnp.concatenate([came[2 * p][...], came[2 * p + 1][...]], axis=1)
        grad = (kept[p][...] + sent) * scale
        first_new = 0.9 * moment(p) + 0.1 * grad
        second_new = 0.95 * moment(2 + p) + 0.05 * grad * grad
        update = learning * first_new / (jnp.sqrt(second_new * (1.0 / bias_second)) + 1e-08)
        outs[p][0] = (w_ref[p].astype(jnp.float32) - update).astype(jnp.bfloat16)
        outs[2 + p][0] = first_new.astype(jnp.bfloat16)
        outs[4 + p][0] = second_new.astype(jnp.bfloat16)


def adam(here, winner, rate, weights, got, mine, other, scale):
    hidden, width = weights.shape[1], weights.shape[2]
    rows = 32
    pair = pl.BlockSpec((2, rows, width), lambda i, *_: (0, i, 0))
    four = pl.BlockSpec((4, rows, width // 2), lambda i, *_: (0, i, 0))
    flat = pl.BlockSpec((rows, width), lambda i, *_: (i, 0))
    piece = pl.BlockSpec((rows, width // 2), lambda i, *_: (i, 0))
    one = pl.BlockSpec((1, rows, width), lambda i, *_: (0, i, 0))
    return pl.pallas_call(
        functools.partial(adam_kernel, scale),
        grid_spec=pltpu.PrefetchScalarGridSpec(
            num_scalar_prefetch=3,
            grid=(hidden // rows,),
            in_specs=[pair] + [four] * 2 + [flat] * 2 + [piece] * 4,
            out_specs=[one] * 6,
        ),
        out_shape=[jax.ShapeDtypeStruct((1, hidden, width), jnp.bfloat16)] * 6,
        compiler_params=pltpu.CompilerParams(vmem_limit_bytes=60 * 2**20),
    )(here, winner, rate, weights, *got, *mine, *other)


def losers(winner):
    low, high = 0, 0
    for m in range(7, -1, -1):
        low = jnp.where(winner[m] != m, m, low)
    for m in range(8):
        high = jnp.where(winner[m] != m, m, high)
    return low, high


def route(mode, here, winner):
    member = here[0]
    column, row = member // 2, member % 2
    low, high = losers(winner)
    if mode == "cross":
        return [(column - winner[m] // 2 + 4) % 4 for m in (low, high)]
    if mode == "place":
        return [moved(here, winner, part) for part in range(4)]
    wanted = []
    for j in range(4):
        target = j * 2 + row if mode == "columns" else ((column + j) % 4) * 2 + row
        source = winner[target]
        inside = (column - source // 2 + 4) % 4
        outside = jnp.where(target == low, 4, 5)
        wanted.append(jnp.where(source % 2 == row, inside, outside))
    return wanted


def pick_kernel(mode, span, here, winner, *refs):
    count = 2 if mode == "cross" else 4
    stage, sems = refs[-2:]
    if mode == "gather":
        outs, refs = list(refs[-6:-2]), list(refs[:-6])
    else:
        outs, refs = [refs[-3].at[k] for k in range(count)], list(refs[:-3])
    came = []
    if mode in ("gather", "columns"):
        last = refs.pop()
        came = [last.at[0], last.at[1]]
    choices = [ref.at[:, pl.ds(span[0], span[1])] if span else ref for ref in refs] + came
    index = route(mode, here, winner)
    for k in range(count):
        for i, ref in enumerate(choices):

            @pl.when(index[k] == i)
            def _():
                pltpu.make_async_copy(ref, stage.at[k], sems.at[k]).start()

    for k in range(count):
        pltpu.make_async_copy(choices[0], stage.at[k], sems.at[k]).wait()
        pltpu.make_async_copy(stage.at[k], outs[k], sems.at[4 + k]).start()
    for k in range(count):
        pltpu.make_async_copy(stage.at[k], outs[k], sems.at[4 + k]).wait()


def pick(mode, here, winner, arrays, span=None):
    rows, width = arrays[0].shape
    shape = (rows, span[1] if span else width)
    kind = arrays[0].dtype
    count = 2 if mode == "cross" else 4
    smem = pl.BlockSpec(memory_space=pltpu.SMEM)
    anywhere = pl.BlockSpec(memory_space=pl.ANY)
    if mode == "gather":
        out_shape, out_specs = [jax.ShapeDtypeStruct(shape, kind)] * 4, [anywhere] * 4
    else:
        out_shape, out_specs = jax.ShapeDtypeStruct((count,) + shape, kind), anywhere
    return pl.pallas_call(
        functools.partial(pick_kernel, mode, span),
        in_specs=[smem, smem] + [anywhere] * len(arrays),
        out_specs=out_specs,
        out_shape=out_shape,
        scratch_shapes=[
            pltpu.VMEM((count,) + shape, kind),
            pltpu.SemaphoreType.DMA((8,)),
        ],
        compiler_params=pltpu.CompilerParams(vmem_limit_bytes=60 * 2**20),
        cost_estimate=pl.CostEstimate(
            flops=0, bytes_accessed=4 * count * arrays[0].size, transcendentals=0
        ),
    )(here, winner, *arrays)


def spread(pieces):
    return [lax.ppermute(pieces[j], "member", along_row(j)) for j in (1, 2, 3)]


def body(
    tokens,
    cotangent,
    gate_weight,
    up_weight,
    gate_first,
    up_first,
    gate_second,
    up_second,
    winner,
    rate_index,
):
    sync = lax.optimization_barrier
    own = tokens[0]
    count, width = own.shape
    hidden = gate_weight.shape[1]
    scale = width ** (-0.5)
    here = jnp.stack([lax.axis_index("member"), lax.axis_index("fsdp")]).astype(jnp.int32)
    learning = 0.2 * jnp.exp2(
        (rate_index[lax.axis_index("member")].astype(jnp.float32) - 2.0) * 0.5
    )
    rate = jnp.full((1,), learning / bias_first, jnp.float32)

    def fsdp(value, pairs):
        return lax.ppermute(value, "fsdp", pairs)

    def exchange(held, span=None):
        return lax.ppermute(pick("cross", here, winner, held, span), "member", row_swap)

    def gathered(held, came):
        sent = pick("gather", here, winner, [*held, came])
        return [sent[0], *spread(sent)]

    def columns(held, came, span):
        return lax.all_to_all(
            pick("columns", here, winner, [*held, came], span),
            "member",
            0,
            0,
            axis_index_groups=rows_of_members,
            tiled=True,
        )

    half = hidden // 2
    spans = [(0, width // 2), (width // 2, width // 2)]
    weights = [w[0, k * half : (k + 1) * half] for w in (gate_weight, up_weight) for k in range(2)]
    moments = [m[0] for m in (gate_first, up_first, gate_second, up_second)]
    with jax.named_scope("tick_a"):
        turned = cotangent[0].T.reshape(16, 2 * hidden, count)
        cots = lax.all_to_all(turned, "fsdp", 0, 0, axis_index_groups=same_core, tiled=True)
        start = jnp.concatenate([own, fsdp(own, low_swap)])
        held0 = [weights[0], *spread(weights)]
    start, held0, moments = sync((start, held0, moments))
    with jax.named_scope("tick_b"):
        up1, down1 = fsdp(start, z_up), fsdp(start, z_down)
        came0 = exchange(held0)
        held1 = [moments[0], *spread(moments)]
    up1, down1, came0, held0, cots = sync((up1, down1, came0, held0, cots))
    with jax.named_scope("tick_c"):
        up2, down2 = fsdp(up1, z_up), fsdp(down1, z_down)
        got0 = gathered(held0, came0)
        sent1 = pick("cross", here, winner, held1, spans[0])
    up2, down2, got0, held1, sent1 = sync((up2, down2, got0, held1, sent1))
    with jax.named_scope("tick_d"):
        up3, down3 = fsdp(up2, z_up), fsdp(down2, z_down)
        came1 = lax.ppermute(sent1, "member", row_swap)
        sent2 = pick("cross", here, winner, held1, spans[1])
        mine = pick("place", here, winner, got0).reshape(2, hidden, width)
        theirs = fsdp(mine, core_swap)
        sources = [(d, b) for d in (0, -1, 1) for b in range(2)]
        sums = terms(here, mine, theirs, cots, [start, up1, down1], sources, None, scale)
    up3, down3, came1, sums, held1, sent2 = sync((up3, down3, came1, sums, held1, sent2))
    with jax.named_scope("tick_e"):
        sides = [fsdp(up3[:count], z_up), fsdp(down3[count:], z_down)]
        got1 = columns(held1, came1, spans[0])
        came2 = lax.ppermute(sent2, "member", row_swap)
        sources = [(d, b) for d in (-2, 2, -3, 3) for b in range(2)]
        sums = terms(here, mine, theirs, cots, [up2, down2, up3, down3], sources, sums, scale)
    sides, came2, sums, got1, held1 = sync((sides, came2, sums, got1, held1))
    with jax.named_scope("tick_f"):
        got2 = columns(held1, came2, spans[1])
        sources = [(4, b) for b in range(2)]
        sums = terms(here, mine, theirs, cots, sides, sources, sums, scale)
        other = [fsdp(part, core_swap) for part in sums[2:]]
    with jax.named_scope("adam"):
        return tuple(adam(here, winner, rate, mine, [got1, got2], sums[:2], other, scale))


def solution(mesh):
    split = P("member", "fsdp", None)
    return jax.shard_map(
        body,
        mesh=mesh,
        in_specs=(split,) * 8 + (P(), P()),
        out_specs=(split,) * 6,
        check_vma=False,
    )
```

```python
import functools

import jax
import jax.numpy as jnp
from jax import lax
from jax.experimental import pallas as pl
from jax.experimental.pallas import tpu as pltpu
from jax.sharding import PartitionSpec as P

gelu_c = 0.7978845608028654
bias_first = 1.0 - 0.9**10
bias_second = 1.0 - 0.95**10
nz = 8
tile = 256


def device(z, low, core):
    return (z * 2 + low) * 2 + core


everyone = [(z, low, core) for z in range(nz) for low in range(2) for core in range(2)]
z_up = [(device(z, a, c), device((z + 1) % nz, a, c)) for z, a, c in everyone]
z_down = [(b, a) for a, b in z_up]
core_swap = [(i, i ^ 1) for i in range(32)]
same_core = [[i for i in range(32) if i % 2 == core] for core in range(2)]
low_swap = [(i, i ^ 2) for i in range(32)]
row_swap = [(m, m ^ 1) for m in range(8)]


rows_of_members = [[m for m in range(8) if m % 2 == row] for row in range(2)]


def along_row(hops):
    return [(m, (m + 2 * hops) % 8) for m in range(8)]


def gelu_parts(gate_pre):
    tangent = jnp.tanh(gelu_c * (gate_pre + 0.044715 * gate_pre * gate_pre * gate_pre))
    activated = 0.5 * gate_pre * (1.0 + tangent)
    slope = 0.5 * (1.0 + tangent) + 0.5 * gate_pre * (1.0 - tangent * tangent) * gelu_c * (
        1.0 + 3.0 * 0.044715 * gate_pre * gate_pre
    )
    return (activated, slope)


def launch(copies):
    for copy in copies:
        copy.start()
    for copy in copies:
        copy.wait()


def terms_kernel(lengths, sources, first, scale, here, mine, theirs, cots, *refs):
    count = len(lengths)
    tokens, refs = refs[:count], refs[count:]
    if not first:
        kept, sent, refs = refs[:2], refs[2:6], refs[6:]
    keep, send = refs[:2], refs[2:6]
    x, c, w, grad, cot, sems = refs[6:]
    rows, hidden = mine.shape[1], 2 * mine.shape[1]
    half = mine.shape[2] // 2
    me = here[1]
    z, low, core = me // 4, (me // 2) % 2, me % 2
    mine_at = pl.multiple_of(core * rows, 32)
    theirs_at = pl.multiple_of((1 - core) * rows, 32)
    pairs = []
    for p in range(2):
        pairs.append((mine.at[p], w.at[pl.ds(p * hidden + mine_at, rows)]))
        pairs.append((theirs.at[p], w.at[pl.ds(p * hidden + theirs_at, rows)]))
    at = 0
    for ref, length in zip(tokens, lengths):
        pairs.append((ref, x.at[pl.ds(at, length)]))
        at += length
    for k, (hops, other) in enumerate(sources):
        source = ((z + hops + nz) % nz) * 2 + (low + other) % 2
        pairs.append((cots.at[source], c.at[k]))
    ready = len(pairs)
    if not first:
        for p in range(2):
            pairs.append((kept[p], grad.at[pl.ds(p * hidden + mine_at, rows)]))
            for h in range(2):
                to = (pl.ds(p * hidden + theirs_at, rows), pl.ds(h * half, half))
                pairs.append((sent[2 * p + h], grad.at[to]))
    copies = [pltpu.make_async_copy(a, b, sems.at[k]) for k, (a, b) in enumerate(pairs)]
    for copy in copies:
        copy.start()
    for copy in copies[:ready]:
        copy.wait()

    @pl.loop(0, x.shape[0] // tile)
    def _(t):
        block = x[pl.ds(pl.multiple_of(t * tile, tile), tile), :]
        pre = (
            lax.dot_general(
                w[...], block, (((1,), (1,)), ((), ())), preferred_element_type=jnp.float32
            )
            * scale
        )
        value = jnp.concatenate([c[2 * t], c[2 * t + 1]], axis=1).astype(jnp.float32)
        activated, slope = gelu_parts(pre[:hidden])
        columns = pl.ds(pl.multiple_of(t * tile, tile), tile)
        cot[pl.ds(0, hidden), columns] = (value * pre[hidden:] * slope).astype(jnp.bfloat16)
        cot[pl.ds(hidden, hidden), columns] = (value * activated).astype(jnp.bfloat16)

    for copy in copies[ready:]:
        copy.wait()

    @pl.loop(0, x.shape[1] // tile)
    def _(n):
        columns = pl.ds(pl.multiple_of(n * tile, tile), tile)
        part = jnp.dot(cot[...], x[:, columns], preferred_element_type=jnp.float32)
        if first:
            grad[:, columns] = part
        else:
            grad[:, columns] += part

    outs = []
    for p in range(2):
        for h in range(2):
            to = (pl.ds(p * hidden + theirs_at, rows), pl.ds(h * half, half))
            outs.append((grad.at[to], send[2 * p + h]))
        outs.append((grad.at[pl.ds(p * hidden + mine_at, rows)], keep[p]))
    launch([pltpu.make_async_copy(a, b, sems.at[k]) for k, (a, b) in enumerate(outs)])


def terms(here, mine, theirs, cots, blocks, sources, totals, scale):
    rows, width = mine.shape[1], mine.shape[2]
    total = sum(b.shape[0] for b in blocks)
    first = totals is None
    anywhere = pl.BlockSpec(memory_space=pl.ANY)
    args = [mine, theirs, cots, *blocks, *([] if first else totals)]
    sums = jax.ShapeDtypeStruct((rows, width), jnp.float32)
    parts = jax.ShapeDtypeStruct((rows, width // 2), jnp.float32)
    kernel = functools.partial(
        terms_kernel, tuple(b.shape[0] for b in blocks), tuple(sources), first, scale
    )
    return pl.pallas_call(
        kernel,
        in_specs=[pl.BlockSpec(memory_space=pltpu.SMEM)] + [anywhere] * len(args),
        out_specs=[anywhere] * 6,
        out_shape=[sums] * 2 + [parts] * 4,
        scratch_shapes=[
            pltpu.VMEM((total, width), jnp.bfloat16),
            pltpu.VMEM((len(sources), 2 * rows, cots.shape[2]), jnp.bfloat16),
            pltpu.VMEM((4 * rows, width), jnp.bfloat16),
            pltpu.VMEM((4 * rows, width), jnp.float32),
            pltpu.VMEM((4 * rows, total), jnp.bfloat16),
            pltpu.SemaphoreType.DMA((10 + len(blocks) + len(sources),)),
        ],
        compiler_params=pltpu.CompilerParams(vmem_limit_bytes=60 * 2**20),
        cost_estimate=pl.CostEstimate(
            flops=16 * rows * width * total,
            bytes_accessed=20 * 2**20,
            transcendentals=2 * rows * total,
        ),
    )(here, *args)


def moved(here, winner, part):
    source = winner[here[0]]
    return (here[0] // 2 - source // 2 - part + 8) % 4


def adam_kernel(scale, here, winner, rate, w_ref, *refs):
    got, kept, came, outs = refs[:2], refs[2:4], refs[4:8], refs[8:]
    learning = rate[0]
    column = winner[here[0]] // 2

    def moment(part):
        which = (column + part) % 4
        return jnp.concatenate([got[0][which], got[1][which]], axis=1).astype(jnp.float32)

    for p in range(2):
        sent = jnp.concatenate([came[2 * p][...], came[2 * p + 1][...]], axis=1)
        grad = (kept[p][...] + sent) * scale
        first_new = 0.9 * moment(p) + 0.1 * grad
        second_new = 0.95 * moment(2 + p) + 0.05 * grad * grad
        update = learning * first_new / (jnp.sqrt(second_new * (1.0 / bias_second)) + 1e-08)
        outs[p][0] = (w_ref[p].astype(jnp.float32) - update).astype(jnp.bfloat16)
        outs[2 + p][0] = first_new.astype(jnp.bfloat16)
        outs[4 + p][0] = second_new.astype(jnp.bfloat16)


def adam(here, winner, rate, weights, got, mine, other, scale):
    hidden, width = weights.shape[1], weights.shape[2]
    rows = 32
    pair = pl.BlockSpec((2, rows, width), lambda i, *_: (0, i, 0))
    four = pl.BlockSpec((4, rows, width // 2), lambda i, *_: (0, i, 0))
    flat = pl.BlockSpec((rows, width), lambda i, *_: (i, 0))
    piece = pl.BlockSpec((rows, width // 2), lambda i, *_: (i, 0))
    one = pl.BlockSpec((1, rows, width), lambda i, *_: (0, i, 0))
    return pl.pallas_call(
        functools.partial(adam_kernel, scale),
        grid_spec=pltpu.PrefetchScalarGridSpec(
            num_scalar_prefetch=3,
            grid=(hidden // rows,),
            in_specs=[pair] + [four] * 2 + [flat] * 2 + [piece] * 4,
            out_specs=[one] * 6,
        ),
        out_shape=[jax.ShapeDtypeStruct((1, hidden, width), jnp.bfloat16)] * 6,
        compiler_params=pltpu.CompilerParams(vmem_limit_bytes=60 * 2**20),
    )(here, winner, rate, weights, *got, *mine, *other)


def losers(winner):
    low, high = 0, 0
    for m in range(7, -1, -1):
        low = jnp.where(winner[m] != m, m, low)
    for m in range(8):
        high = jnp.where(winner[m] != m, m, high)
    return low, high


def route(mode, here, winner):
    member = here[0]
    column, row = member // 2, member % 2
    low, high = losers(winner)
    if mode == "cross":
        return [(column - winner[m] // 2 + 4) % 4 for m in (low, high)]
    if mode == "place":
        return [moved(here, winner, part) for part in range(4)]
    wanted = []
    for j in range(4):
        target = j * 2 + row if mode == "columns" else ((column + j) % 4) * 2 + row
        source = winner[target]
        inside = (column - source // 2 + 4) % 4
        outside = jnp.where(target == low, 4, 5)
        wanted.append(jnp.where(source % 2 == row, inside, outside))
    return wanted


def pick_kernel(mode, span, here, winner, *refs):
    count = 2 if mode == "cross" else 4
    stage, sems = refs[-2:]
    if mode == "gather":
        outs, refs = list(refs[-6:-2]), list(refs[:-6])
    else:
        outs, refs = [refs[-3].at[k] for k in range(count)], list(refs[:-3])
    came = []
    if mode in ("gather", "columns"):
        last = refs.pop()
        came = [last.at[0], last.at[1]]
    choices = [ref.at[:, pl.ds(span[0], span[1])] if span else ref for ref in refs] + came
    index = route(mode, here, winner)
    for k in range(count):
        for i, ref in enumerate(choices):

            @pl.when(index[k] == i)
            def _():
                pltpu.make_async_copy(ref, stage.at[k], sems.at[k]).start()

    for k in range(count):
        pltpu.make_async_copy(choices[0], stage.at[k], sems.at[k]).wait()
        pltpu.make_async_copy(stage.at[k], outs[k], sems.at[4 + k]).start()
    for k in range(count):
        pltpu.make_async_copy(stage.at[k], outs[k], sems.at[4 + k]).wait()


def pick(mode, here, winner, arrays, span=None):
    rows, width = arrays[0].shape
    shape = (rows, span[1] if span else width)
    kind = arrays[0].dtype
    count = 2 if mode == "cross" else 4
    smem = pl.BlockSpec(memory_space=pltpu.SMEM)
    anywhere = pl.BlockSpec(memory_space=pl.ANY)
    if mode == "gather":
        out_shape, out_specs = [jax.ShapeDtypeStruct(shape, kind)] * 4, [anywhere] * 4
    else:
        out_shape, out_specs = jax.ShapeDtypeStruct((count,) + shape, kind), anywhere
    return pl.pallas_call(
        functools.partial(pick_kernel, mode, span),
        in_specs=[smem, smem] + [anywhere] * len(arrays),
        out_specs=out_specs,
        out_shape=out_shape,
        scratch_shapes=[
            pltpu.VMEM((count,) + shape, kind),
            pltpu.SemaphoreType.DMA((8,)),
        ],
        compiler_params=pltpu.CompilerParams(vmem_limit_bytes=60 * 2**20),
        cost_estimate=pl.CostEstimate(
            flops=0, bytes_accessed=4 * count * arrays[0].size, transcendentals=0
        ),
    )(here, winner, *arrays)


def spread(pieces):
    return [lax.ppermute(pieces[j], "member", along_row(j)) for j in (1, 2, 3)]


def body(
    tokens,
    cotangent,
    gate_weight,
    up_weight,
    gate_first,
    up_first,
    gate_second,
    up_second,
    winner,
    rate_index,
):
    sync = lax.optimization_barrier
    own = tokens[0]
    count, width = own.shape
    hidden = gate_weight.shape[1]
    scale = width ** (-0.5)
    here = jnp.stack([lax.axis_index("member"), lax.axis_index("fsdp")]).astype(jnp.int32)
    learning = 0.2 * jnp.exp2(
        (rate_index[lax.axis_index("member")].astype(jnp.float32) - 2.0) * 0.5
    )
    rate = jnp.full((1,), learning / bias_first, jnp.float32)

    def fsdp(value, pairs):
        return lax.ppermute(value, "fsdp", pairs)

    def exchange(held, span=None):
        return lax.ppermute(pick("cross", here, winner, held, span), "member", row_swap)

    def gathered(held, came):
        sent = pick("gather", here, winner, [*held, came])
        return [sent[0], *spread(sent)]

    def columns(held, came, span):
        return lax.all_to_all(
            pick("columns", here, winner, [*held, came], span),
            "member",
            0,
            0,
            axis_index_groups=rows_of_members,
            tiled=True,
        )

    half = hidden // 2
    spans = [(0, width // 2), (width // 2, width // 2)]
    weights = [w[0, k * half : (k + 1) * half] for w in (gate_weight, up_weight) for k in range(2)]
    moments = [m[0] for m in (gate_first, up_first, gate_second, up_second)]
    with jax.named_scope("tick_a"):
        turned = cotangent[0].T.reshape(16, 2 * hidden, count)
        cots = lax.all_to_all(turned, "fsdp", 0, 0, axis_index_groups=same_core, tiled=True)
        start = jnp.concatenate([own, fsdp(own, low_swap)])
        held0 = [weights[0], *spread(weights)]
    start, held0, moments = sync((start, held0, moments))
    with jax.named_scope("tick_b"):
        up1, down1 = fsdp(start, z_up), fsdp(start, z_down)
        came0 = exchange(held0)
        held1 = [moments[0], *spread(moments)]
    up1, down1, came0, held0, cots = sync((up1, down1, came0, held0, cots))
    with jax.named_scope("tick_c"):
        up2, down2 = fsdp(up1, z_up), fsdp(down1, z_down)
        got0 = gathered(held0, came0)
        sent1 = pick("cross", here, winner, held1, spans[0])
    up2, down2, got0, held1, sent1 = sync((up2, down2, got0, held1, sent1))
    with jax.named_scope("tick_d"):
        up3, down3 = fsdp(up2, z_up), fsdp(down2, z_down)
        came1 = lax.ppermute(sent1, "member", row_swap)
        sent2 = pick("cross", here, winner, held1, spans[1])
        mine = pick("place", here, winner, got0).reshape(2, hidden, width)
        theirs = fsdp(mine, core_swap)
        sources = [(d, b) for d in (0, -1, 1) for b in range(2)]
        sums = terms(here, mine, theirs, cots, [start, up1, down1], sources, None, scale)
    up3, down3, came1, sums, held1, sent2 = sync((up3, down3, came1, sums, held1, sent2))
    with jax.named_scope("tick_e"):
        sides = [fsdp(up3[:count], z_up), fsdp(down3[count:], z_down)]
        got1 = columns(held1, came1, spans[0])
        came2 = lax.ppermute(sent2, "member", row_swap)
        sources = [(d, b) for d in (-2, 2) for b in range(2)]
        sums = terms(here, mine, theirs, cots, [up2, down2], sources, sums, scale)
    sides, came2, sums, got1, held1 = sync((sides, came2, sums, got1, held1))
    with jax.named_scope("tick_f"):
        got2 = columns(held1, came2, spans[1])
        sources = [(d, b) for d in (-3, 3, 4) for b in range(2)]
        sums = terms(here, mine, theirs, cots, [up3, down3, *sides], sources, sums, scale)
        other = [fsdp(part, core_swap) for part in sums[2:]]
    with jax.named_scope("adam"):
        return tuple(adam(here, winner, rate, mine, [got1, got2], sums[:2], other, scale))


def solution(mesh):
    split = P("member", "fsdp", None)
    return jax.shard_map(
        body,
        mesh=mesh,
        in_specs=(split,) * 8 + (P(), P()),
        out_specs=(split,) * 6,
        check_vma=False,
    )
```
